256 devices in a mesh: node: 32 (over x, y, core), rows: 8 (over z).
Axes of the slice: x: 4, y: 4, z: 8, core: 2. Of those that a mesh axis runs over, the one named last changes fastest.
Arguments:
- embeddings: bfloat16 [524288, 1024], P(('node', 'rows'))
- membership: int32 [8192, 1], P(('node', 'rows')), may hold values from 0 to 31; in each aligned block of 32 rows (0 to 31, 32 to 63, ...) at most 2 rows name the same one
- start: float32 [32, 16, 1024], P('node'), may hold values from -6 to 6
Outputs:
- directions: float32 [32, 16, 1024], P('node')
- coords: bfloat16 [16, 524288], P(None, ('node', 'rows'))
The draws below stay inside these ranges and needn't reach their ends.
Inputs may be any that keep to these rules, and one draw needn't show every extreme that they name: `membership`: the 32 blocks of one device name each node at most 2 times; some node is named exactly 2 times; every node is named by some block.
All inputs are finite; a program needn't handle non-finite values.
Results may differ from the reference program's by a relative error of at most 0.0015.
Values may be sent and summed in bfloat16 or wider, within the bound.
A program may use at most 64 MiB of HBM per device.

```python
import math
import jax
import jax.numpy as jnp
import numpy as np
from jax import lax

D = 1024
DIRS = 16
BLOCK = 64
PASSES = 3
BPD = 32
MOST = 2
NODES = 32
BLOCKS_ALL = 8192
ROWS_ALL = 524288


def draw_embeddings(key, part):
    key = jax.random.fold_in(key, 11)
    first, second = jax.random.split(key, 2)
    logs = jax.random.uniform(second, (1, D), jnp.float32, math.log(0.3), math.log(3.0))
    scales = jnp.exp(logs)
    values = jax.random.normal(first, (ROWS_ALL, D), jnp.float32)
    return (values * scales).astype(jnp.bfloat16)


def steps_of(stream_key, shape, cuts, low, top_value):
    loudness = 1.0
    for dim, shards_of in cuts:
        heights = jax.random.uniform(jax.random.fold_in(jax.random.fold_in(stream_key, 6), dim), (shards_of,), jnp.float32, low / len(cuts), top_value / len(cuts))
        loudness = loudness * jnp.repeat(jnp.exp(heights), shape[dim] // shards_of).reshape((-1,) + (1,) * (len(shape) - 1 - dim))
    return loudness


def routed_block(own_key, own, number, rows, amount, top, reach, slope):
    ranking = jax.random.permutation(own_key, amount)
    packed, common = portions_of(amount, rows * top, reach, slope, True), portions_of(amount, rows * top, reach, slope, False)
    places = jnp.arange(amount)

    def named(sizes, offset_by):
        used = int((sizes > 0).sum())
        fixed = max(1, used // 4)
        passed = fixed + (places - fixed + offset_by * (used - fixed)) % max(1, amount - fixed)
        return jnp.zeros((amount,), jnp.int32).at[ranking[jnp.where(places < fixed, places, passed)]].set(jnp.asarray(sizes, jnp.int32))

    sizes = jnp.where(number % 4 == 0, named(packed, number // 4), named(common, number - number // 4 - 1))
    mixed = jax.random.permutation(jax.random.fold_in(own, 3), amount)
    donor, sink = mixed[0:amount // 2 * 2:2], mixed[1:amount // 2 * 2:2]
    margin = jnp.minimum(sizes[donor] - 1, reach - sizes[sink]) // 2
    margin = jnp.where((donor == ranking[0]) | (sink == ranking[0]) | (sizes[sink] == 0), 0, jnp.maximum(margin, 0))
    passed = jax.random.randint(jax.random.fold_in(own, 4), (amount // 2,), 0, 1 << 20) % (margin + 1)
    sizes = sizes.at[donor].add(-passed).at[sink].add(passed)
    items = jnp.searchsorted(jnp.cumsum(sizes), jnp.arange(rows * top), side="right").astype(jnp.int32)
    listing = items.reshape(top, rows).T
    listing = listing[jax.random.permutation(jax.random.fold_in(own, 1), rows)]
    offset_by = jax.random.randint(jax.random.fold_in(own, 2), (rows, 1), 0, top)
    return jnp.take_along_axis(listing, (jnp.arange(top)[None, :] + offset_by) % top, axis=1)


def portions_of(count, total, bound, slope, full):
    loads = [(1 << 20) // math.isqrt(grade ** slope) + 1 for grade in range(1, count + 1)]
    largest = bound if full else min(bound, max(-(-total // count), total * loads[0] // sum(loads)))
    least = 1 if total - largest >= count - 1 else 0
    holding, rest = [largest] + [least] * (count - 1), total - largest - least * (count - 1)
    while rest > 0:
        candidates = [i for i in range(1, count) if holding[i] < largest] or [i for i in range(1, count) if holding[i] < bound]
        whole, left = sum([loads[i] for i in candidates]), rest
        for i in candidates:
            extra = min(bound - holding[i], max(1, left * loads[i] // whole), rest)
            holding[i] = holding[i] + extra
            rest = rest - extra
    return np.array(holding)


def centred(rng, shape, spread, most, pieces=(), kind=jnp.bfloat16):
    factor_of = steps_of(rng, shape, pieces, -0.22, 0.18) if pieces else 1.0
    values = jax.random.normal(rng, shape, jnp.float32) * spread * factor_of
    return jnp.minimum(jnp.maximum(values, -most), most).astype(kind)


def setup_inputs(seed: int = 0) -> dict:
    arg_keys = jax.random.split(jax.random.key(seed), 4)
    embeddings = draw_embeddings(jax.random.fold_in(arg_keys[3], 71), 0)
    membership_keys = jax.random.split(jax.random.fold_in(arg_keys[1], 1), BLOCKS_ALL // BPD)
    membership_turns = jax.random.permutation(jax.random.fold_in(arg_keys[1], 3), BLOCKS_ALL // BPD)
    membership = jax.vmap(lambda own, number: routed_block(jax.random.fold_in(arg_keys[1], 2), own, number, BPD, NODES, 1, MOST, 2))(membership_keys, membership_turns).reshape((BLOCKS_ALL, 1))
    start = centred(arg_keys[2], (NODES, DIRS, D), 1.0, 6.0, ((0, 32),), jnp.float32)
    return {"embeddings": embeddings, "membership": membership, "start": start}


def orthonormal(matrix):
    square = jnp.dot(matrix, matrix.T, precision=lax.Precision.HIGHEST)
    factor = jnp.linalg.cholesky(square)
    return lax.linalg.triangular_solve(factor, matrix, left_side=True, lower=True)

def reference(embeddings, membership, start):
    member = membership[:, 0]
    blocks = embeddings.reshape(BLOCKS_ALL, BLOCK, D)
    order = jnp.argsort(member, stable=True).astype(jnp.int32)
    counts = jnp.sum((member[None, :] == jnp.arange(NODES, dtype=jnp.int32)[:, None]).astype(jnp.int32), axis=1)
    offsets = (jnp.cumsum(counts) - counts).astype(jnp.int32)

    def node_stats(index):

        def accumulate(step, carry):
            gram_sum, row_sum = carry
            chosen = blocks[order[offsets[index] + step]]
            gram_sum = gram_sum + lax.dot_general(chosen.astype(jnp.float32), chosen.astype(jnp.float32), (((0,), (0,)), ((), ())), preferred_element_type=jnp.float32)
            row_sum = row_sum + jnp.sum(chosen.astype(jnp.float32), axis=0)
            return (gram_sum, row_sum)
        init = (jnp.zeros((D, D), jnp.float32), jnp.zeros((D,), jnp.float32))
        gram_sum, row_sum = lax.fori_loop(0, counts[index], accumulate, init)
        node_size = (counts[index] * BLOCK).astype(jnp.float32)
        mean = row_sum / node_size
        cov = gram_sum / node_size - mean[:, None] * mean[None, :]
        vectors = start[index]
        for sweep in range(PASSES):
            vectors = orthonormal(jnp.dot(vectors, cov, precision=lax.Precision.HIGHEST))
        return (vectors, mean)
    directions, means = lax.map(node_stats, jnp.arange(NODES, dtype=jnp.int32))

    def project(pair):
        chosen, owner = pair
        vectors = directions[owner]
        shifted = jnp.dot(vectors, means[owner], precision=lax.Precision.HIGHEST)
        values = jnp.dot(vectors, chosen.astype(jnp.float32).T, precision=lax.Precision.HIGHEST) - shifted[:, None]
        return values.astype(jnp.bfloat16)
    projected = lax.map(project, (blocks, member))
    coords = projected.transpose(1, 0, 2).reshape(DIRS, ROWS_ALL)
    return (directions, coords)
```

```python
import functools

import jax
import jax.numpy as jnp
from jax import lax
from jax.experimental import pallas as pl
from jax.experimental.pallas import tpu as pltpu
from jax.sharding import PartitionSpec as P

PASSES = 3
MESH = pl.DeviceIdType.MESH
F32 = jnp.float32
BF16 = jnp.bfloat16

DIRS = 16
D = 1024
EXT = 128
WIDE = D + EXT
CUT = 640
ROWS = 2048
BLOCK = 64
BLOCKS = 32
TILE = 256
PER = TILE // BLOCK
NX, NY, NZ = 4, 4, 8


def split3(v):
    hi = v.astype(BF16)
    rest = v - hi.astype(F32)
    mid = rest.astype(BF16)
    lo = (rest - mid.astype(F32)).astype(BF16)
    return hi, mid, lo


def kernel(
    member, first, second, x_hbm, start, dirs, coords,
    xv, vall, wblk, acc, sendc, recvc, r1, r2, b1, b2, r3, r4, cc, r5, r6, ff,
    xsem, ag_a1s, ag_a1r, ag_a2s, ag_a2r, ag_b1s, ag_b1r, ag_b2s, ag_b2r, ag_cs, ag_cr,
    rs_cs, rs_cr, rs_1s, rs_1r, rs_2s, rs_2r, rs_3s, rs_3r, rs_4s, rs_4r,
    z_1s, z_1r, z_2s, z_2r, z_3s, z_3r,
):
    me = lax.axis_index("node")
    z = lax.axis_index("rows")
    x, y, c = me // 8, (me // 2) % 4, me % 2

    def at(x_, y_, c_):
        return (x_ * 8 + y_ * 2 + c_, z)

    def along_x(d):
        return at((x + d) % NX, y, c)

    def along_y(d):
        return at(x, (y + d) % NY, c)

    def along_z(d):
        return (me, (z + d) % NZ)

    partner = at(x, y, 1 - c)

    def send(src, dst, ssem, rsem, to):
        return pltpu.make_async_remote_copy(
            src_ref=src, dst_ref=dst, send_sem=ssem, recv_sem=rsem, device_id=to, device_id_type=MESH
        )

    load = pltpu.make_async_copy(x_hbm, xv, xsem)
    load.start()

    barrier = pltpu.get_barrier_semaphore()
    peers = [partner]
    peers += [along_x(d) for d in range(1, NX)]
    peers += [along_y(d) for d in range(1, NY)]
    peers += [along_z(d) for d in range(1, NZ)]
    for peer in peers:
        pl.semaphore_signal(barrier, inc=1, device_id=peer, device_id_type=MESH)
    pl.semaphore_wait(barrier, len(peers))

    vall[x, y, c, :, 0:D] = start[...]
    vall[x, y, c, :, D:WIDE] = jnp.zeros((DIRS, EXT), F32)
    wblk[BLOCKS] = jnp.zeros((DIRS, WIDE), F32)

    def gather():
        one = lambda a, b, lo, hi: vall.at[a, b, c, :, lo:hi]
        row = lambda a: vall.at[a, :, c, :, 0:CUT]
        col = lambda b: vall.at[:, b, c, :, CUT:WIDE]
        sent, core = [], []
        for d in range(1, 4):
            own = one(x, y, 0, CUT)
            sent.append(send(own, own, ag_a1s.at[d - 1], ag_a1r.at[d - 1], along_y(d)))
            own = one(x, y, CUT, WIDE)
            sent.append(send(own, own, ag_a2s.at[d - 1], ag_a2r.at[d - 1], along_x(d)))
        for cp in sent:
            cp.start()

        def hand(ref):
            i = len(core)
            core.append(send(ref, ref, ag_cs.at[i], ag_cr.at[i], partner))
            core[-1].start()

        hand(vall.at[x, y, c])
        for cp in sent:
            cp.wait_recv()
        later = []
        for d in range(1, 4):
            later.append(send(row(x), row(x), ag_b1s.at[d - 1], ag_b1r.at[d - 1], along_x(d)))
            later.append(send(col(y), col(y), ag_b2s.at[d - 1], ag_b2r.at[d - 1], along_y(d)))
        for cp in later:
            cp.start()
        for d in range(1, 4):
            hand(one(x, (y - d) % NY, 0, CUT))
            hand(one((x - d) % NX, y, CUT, WIDE))
        for d in range(1, 4):
            later[2 * d - 2].wait_recv()
            hand(row((x - d) % NX))
            later[2 * d - 1].wait_recv()
            hand(col((y - d) % NY))
        for cp in core:
            cp.wait_recv()
        for cp in sent + later + core:
            cp.wait_send()

    group = lax.broadcasted_iota(jnp.int32, (DIRS, TILE), 1) >> 6

    def project(t):
        tile = xv[pl.ds(pl.multiple_of(t * TILE, TILE), TILE), :]
        parts, shifts = [], []
        for i in range(PER):
            m = member[PER * t + i]
            parts += split3(vall[m // 8, (m // 2) % 4, m % 2, :, 0:D])
            shifts.append(vall[m // 8, (m // 2) % 4, m % 2, :, D:WIDE])
        stack = jnp.concatenate(parts, axis=0)
        p3 = lax.dot_general(stack, tile, (((1,), (1,)), ((), ())), preferred_element_type=F32)
        out = []
        for i in range(PER):
            a = 3 * DIRS * i
            p = (p3[a + 2 * DIRS : a + 3 * DIRS] + p3[a + DIRS : a + 2 * DIRS]) + p3[a : a + DIRS]
            p = p - jnp.concatenate([shifts[i], shifts[i]], axis=1)
            out.append(jnp.where(group == i, p, 0.0))
        return tile, out

    ones_rows = (
        lax.broadcasted_iota(jnp.int32, (DIRS, TILE), 0) == group
    ).astype(F32).astype(BF16)

    def tile_step(t, carry):
        tile, ps = project(t)
        stack = []
        for p in ps:
            stack += split3(p)
        stack.append(ones_rows)
        w3 = jnp.dot(jnp.concatenate(stack, axis=0), tile, preferred_element_type=F32)
        for i in range(PER):
            a = 3 * DIRS * i
            b = PER * t + i
            wblk[b, :, 0:D] = (
                w3[a + 2 * DIRS : a + 3 * DIRS] + w3[a + DIRS : a + 2 * DIRS]
            ) + w3[a : a + DIRS]
            s = 3 * DIRS * PER + i
            for r in range(8):
                wblk[b, r : r + 1, D:WIDE] = w3[s : s + 1, 128 * r : 128 * (r + 1)]
            wblk[b, 8:16, D:WIDE] = jnp.full((8, EXT), float(BLOCK), F32)
        return carry

    def scatter():
        def for_partner(i, carry):
            a, b = i // NY, i % NY
            j = i * 2 + (1 - c)
            sendc[a, b] = wblk[first[j]] + wblk[second[j]]
            return carry

        def for_own(i, carry):
            a, b = i // NY, i % NY
            j = i * 2 + c
            acc[a, b] = wblk[first[j]] + wblk[second[j]]
            return carry

        lax.fori_loop(0, 16, for_partner, 0)
        over = send(sendc, recvc, rs_cs, rs_cr, partner)
        over.start()
        lax.fori_loop(0, 16, for_own, 0)
        over.wait_recv()

        def add_core(i, carry):
            a, b = i // NY, i % NY
            acc[a, b] = acc[a, b] + recvc[a, b]
            return carry

        lax.fori_loop(0, 16, add_core, 0)
        sent = []
        for d in range(1, 4):
            sent.append(send(acc.at[(x + d) % NX, :, :, 0:CUT], r1.at[d - 1],
                             rs_1s.at[d - 1], rs_1r.at[d - 1], along_x(d)))
            sent.append(send(acc.at[:, (y + d) % NY, :, CUT:WIDE], r2.at[d - 1],
                             rs_2s.at[d - 1], rs_2r.at[d - 1], along_y(d)))
        for cp in sent:
            cp.start()
        for cp in sent:
            cp.wait_recv()
        for q in range(4):
            b1[q] = (acc[x, q, :, 0:CUT] + r1[0, q]) + (r1[1, q] + r1[2, q])
            b2[q] = (acc[q, y, :, CUT:WIDE] + r2[0, q]) + (r2[1, q] + r2[2, q])
        later = []
        for d in range(1, 4):
            later.append(send(b1.at[(y + d) % NY], r3.at[d - 1],
                              rs_3s.at[d - 1], rs_3r.at[d - 1], along_y(d)))
            later.append(send(b2.at[(x + d) % NX], r4.at[d - 1],
                              rs_4s.at[d - 1], rs_4r.at[d - 1], along_x(d)))
        for cp in later:
            cp.start()
        for cp in later:
            cp.wait_recv()
        cc[:, 0:CUT] = (b1[y] + r3[0]) + (r3[1] + r3[2])
        cc[:, CUT:WIDE] = (b2[x] + r4[0]) + (r4[1] + r4[2])
        r6[z] = cc[:, D:WIDE]
        ring = []
        for d in range(1, NZ):
            there = pl.ds(pl.multiple_of(((z + d) % NZ) * 128, 128), 128)
            ring.append(send(cc.at[:, there], r5.at[d - 1], z_1s.at[d - 1], z_1r.at[d - 1], along_z(d)))
            ring.append(send(cc.at[:, D:WIDE], r6.at[z], z_2s.at[d - 1], z_2r.at[d - 1], along_z(d)))
        for cp in ring:
            cp.start()
        for cp in ring:
            cp.wait_recv()
        here = pl.ds(pl.multiple_of(z * 128, 128), 128)
        part = cc[:, here]
        for d in range(NZ - 1):
            part = part + r5[d]
        extra = r6[0]
        for d in range(1, NZ):
            extra = extra + r6[d]
        ff[:, here] = part
        back = []
        for d in range(1, NZ):
            back.append(send(ff.at[:, here], ff.at[:, here], z_3s.at[d - 1], z_3r.at[d - 1], along_z(d)))
        for cp in back:
            cp.start()
        for cp in back:
            cp.wait_recv()
        for cp in [over] + sent + later + ring + back:
            cp.wait_send()
        return extra

    row_id = lax.broadcasted_iota(jnp.int32, (DIRS, 1), 0)

    def one_pass(step, carry):
        gather()

        @pl.when(step == 0)
        def _():
            load.wait()

        lax.fori_loop(0, ROWS // TILE, tile_step, 0)
        extra = scatter()
        size = extra[8:9, :]
        mean = extra[0:8, :] / size
        mean_row = jnp.concatenate([mean[r : r + 1] for r in range(8)], axis=1)
        size_row = jnp.concatenate([size] * 8, axis=1)
        old = vall[x, y, c, :, 0:D]
        offset = jnp.where(step == 0, jnp.sum(old * mean_row, axis=1, keepdims=True), 0.0)
        w = ff[...] / size_row - offset * mean_row
        g = lax.dot_general(w, w, (((1,), (1,)), ((), ())), precision=lax.Precision.HIGHEST,
                            preferred_element_type=F32)
        scale = jnp.zeros((DIRS, 1), F32)
        for k in range(DIRS):
            pivot = g[k : k + 1, k : k + 1]
            f = jnp.where(row_id > k, g[:, k : k + 1] / pivot, 0.0)
            scale = jnp.where(row_id == k, 1.0 / jnp.sqrt(pivot), scale)
            g = g - f * g[k : k + 1, :]
            w = w - f * w[k : k + 1, :]
        v = w * scale
        vall[x, y, c, :, 0:D] = v
        vall[x, y, c, :, D:WIDE] = jnp.broadcast_to(
            jnp.sum(v * mean_row, axis=1, keepdims=True), (DIRS, EXT)
        )
        return carry

    lax.fori_loop(0, PASSES, one_pass, 0)
    dirs[...] = vall[x, y, c, :, 0:D]
    gather()

    def last(t, carry):
        _, ps = project(t)
        coords[:, pl.ds(pl.multiple_of(t * TILE, TILE), TILE)] = (
            (ps[0] + ps[1]) + (ps[2] + ps[3])
        ).astype(BF16)
        return carry

    lax.fori_loop(0, ROWS // TILE, last, 0)


def on_device(embeddings, membership, start):
    member = membership[:, 0]
    nodes = jnp.arange(32, dtype=jnp.int32)
    blocks = jnp.arange(BLOCKS, dtype=jnp.int32)
    same = member[None, :] == nodes[:, None]
    first = jnp.min(jnp.where(same, blocks[None, :], BLOCKS), axis=1)
    second = jnp.max(jnp.where(same, blocks[None, :], -1), axis=1)
    second = jnp.where((second < 0) | (second == first), BLOCKS, second)
    smem = pl.BlockSpec(memory_space=pltpu.SMEM)
    vmem = pl.BlockSpec(memory_space=pltpu.VMEM)
    dma = pltpu.SemaphoreType.DMA
    dirs, coords = pl.pallas_call(
        kernel,
        out_shape=(
            jax.ShapeDtypeStruct((DIRS, D), F32),
            jax.ShapeDtypeStruct((DIRS, ROWS), BF16),
        ),
        in_specs=[smem, smem, smem, pl.BlockSpec(memory_space=pl.ANY), vmem],
        out_specs=(vmem, vmem),
        scratch_shapes=[
            pltpu.VMEM((ROWS, D), BF16),
            pltpu.VMEM((NX, NY, 2, DIRS, WIDE), F32),
            pltpu.VMEM((BLOCKS + 1, DIRS, WIDE), F32),
            pltpu.VMEM((NX, NY, DIRS, WIDE), F32),
            pltpu.VMEM((NX, NY, DIRS, WIDE), F32),
            pltpu.VMEM((NX, NY, DIRS, WIDE), F32),
            pltpu.VMEM((3, NY, DIRS, CUT), F32),
            pltpu.VMEM((3, NX, DIRS, WIDE - CUT), F32),
            pltpu.VMEM((NY, DIRS, CUT), F32),
            pltpu.VMEM((NX, DIRS, WIDE - CUT), F32),
            pltpu.VMEM((3, DIRS, CUT), F32),
            pltpu.VMEM((3, DIRS, WIDE - CUT), F32),
            pltpu.VMEM((DIRS, WIDE), F32),
            pltpu.VMEM((NZ - 1, DIRS, 128), F32),
            pltpu.VMEM((NZ, DIRS, EXT), F32),
            pltpu.VMEM((DIRS, D), F32),
            dma,
            dma((3,)), dma((3,)), dma((3,)), dma((3,)),
            dma((3,)), dma((3,)), dma((3,)), dma((3,)),
            dma((13,)), dma((13,)),
            dma, dma,
            dma((3,)), dma((3,)), dma((3,)), dma((3,)),
            dma((3,)), dma((3,)), dma((3,)), dma((3,)),
            dma((7,)), dma((7,)), dma((7,)), dma((7,)), dma((7,)), dma((7,)),
        ],
        compiler_params=pltpu.CompilerParams(
            collective_id=0, has_side_effects=True, vmem_limit_bytes=40 * 1024 * 1024
        ),
    )(member, first, second, embeddings, start[0])
    return (dirs[None], coords)


def solution(mesh):
    return jax.shard_map(
        on_device,
        mesh=mesh,
        in_specs=(P(("node", "rows"), None), P(("node", "rows"), None), P("node", None, None)),
        out_specs=(P("node", None, None), P(None, ("node", "rows"))),
        check_vma=False,
    )
```

```python
import jax
import jax.numpy as jnp
from jax import lax
from jax.experimental import pallas as pl
from jax.experimental.pallas import tpu as pltpu
from jax.sharding import PartitionSpec as P

PASSES = 3
MESH = pl.DeviceIdType.MESH
F32 = jnp.float32
BF16 = jnp.bfloat16
I16 = jnp.int16
I32 = jnp.int32

DIRS = 16
D = 1024
HALF = 512
LANES = 128
KT = HALF // LANES
ROWS = 2048
BLOCK = 64
BLOCKS = 32
TILE = 256
PER = TILE // BLOCK
TILES = ROWS // TILE
CHIPS = 16
NZ = 8


def code(w):
    tiles = [w[:, LANES * k : LANES * (k + 1)] for k in range(KT)]
    top = jnp.maximum(
        jnp.maximum(jnp.abs(tiles[0]), jnp.abs(tiles[1])), jnp.maximum(jnp.abs(tiles[2]), jnp.abs(tiles[3]))
    )
    top = jnp.maximum(jnp.max(top, axis=1, keepdims=True), 1e-30)
    e = jnp.floor(jnp.log2(top))
    scale = jnp.exp2(14.0 - e)
    out = [
        jnp.clip(jnp.round(t * scale), -32767.0, 32767.0).astype(I32).astype(I16) for t in tiles
    ]
    return out, jnp.broadcast_to(e.astype(I32), (DIRS, LANES)).astype(I16)


def put(ref, w):
    out, e = code(w)
    for k in range(KT):
        ref[k] = out[k]
    ref[KT] = e


def scale_of(ref):
    return jnp.exp2(ref[KT].astype(I32).astype(F32) - 14.0)


def kernel(
    member, x_hbm, start, dirs, coords,
    xh, smt, smm, mv, tab, vs, vr, vq, vhl, shift, shift0, shift1, pc, pr, wblk, wq, rq, zq, gs, gr, vout, vin,
    sblk, snode, sr, sz, mm,
    xsem, xs, xr, msem, mss, msr, nsem, tsem, vsem, vss, vsr, h_s, h_r, ag_s, ag_r, p_s, p_r, rs_s, rs_r, z_s, z_r, g_s, g_r,
    ms_s, ms_r, mz_s, mz_r, ma_s, ma_r, o_s, o_r,
):
    me = lax.axis_index("node")
    z = lax.axis_index("rows")
    x, y, c = me >> 3, (me >> 1) & 3, me & 1
    chip = me >> 1
    other = 1 - c

    def chip_at(d):
        return (((x + (d >> 2)) & 3) << 2) + ((y + d) & 3)

    def chip_from(d):
        return (((x + 4 - (d >> 2)) & 3) << 2) + ((y + 4 - (d & 3)) & 3)

    def plane(d):
        return (chip_at(d) * 2 + c, z)

    def column(d):
        return (me, (z + d) & (NZ - 1))

    partner = (chip * 2 + other, z)

    def send(src, dst, ssem, rsem, to):
        return pltpu.make_async_remote_copy(
            src_ref=src, dst_ref=dst, send_sem=ssem, recv_sem=rsem, device_id=to, device_id_type=MESH
        )

    def each(n, what):
        def body(d, carry):
            what(d)
            return carry

        lax.fori_loop(1, n, body, 0)

    mine = pl.ds(pl.multiple_of(c * HALF, HALF), HALF)
    theirs = pl.ds(pl.multiple_of(other * HALF, HALF), HALF)
    load = pltpu.make_async_copy(x_hbm.at[:, mine], xh.at[c], xsem)
    load.start()
    load_m = pltpu.make_async_copy(member, mv.at[c], msem)
    load_m.start()
    load_v = pltpu.make_async_copy(start.at[0], vs, vsem)
    load_v.start()

    barrier = pltpu.get_barrier_semaphore()
    pl.semaphore_signal(barrier, inc=1, device_id=partner, device_id_type=MESH)

    def greet_plane(d):
        pl.semaphore_signal(barrier, inc=1, device_id=plane(d), device_id_type=MESH)

    def greet_column(d):
        pl.semaphore_signal(barrier, inc=1, device_id=column(d), device_id_type=MESH)

    each(CHIPS, greet_plane)
    each(NZ, greet_column)

    group = lax.broadcasted_iota(I32, (DIRS, TILE), 1) >> 6
    ones_rows = (lax.broadcasted_iota(I32, (DIRS, TILE), 0) == group).astype(F32).astype(BF16)

    def sum_tiles(h):
        def body(t, carry):
            tile = xh[h, pl.ds(pl.multiple_of(t * TILE, TILE), TILE), :]
            s = jnp.dot(ones_rows, tile, preferred_element_type=F32)
            for i in range(PER):
                rows = [s[i : i + 1, LANES * k : LANES * (k + 1)] for k in range(KT)]
                rows.append(jnp.full((1, LANES), float(BLOCK), F32))
                rows.append(jnp.zeros((3, LANES), F32))
                sblk[h, PER * t + i] = jnp.concatenate(rows, axis=0)
            return carry

        lax.fori_loop(0, TILES, body, 0)

    wblk[0, BLOCKS] = jnp.zeros((DIRS, HALF), F32)
    wblk[1, BLOCKS] = jnp.zeros((DIRS, HALF), F32)
    sblk[0, BLOCKS] = jnp.zeros((8, LANES), F32)
    sblk[1, BLOCKS] = jnp.zeros((8, LANES), F32)
    load_v.wait()
    put(vq.at[c, chip], vs[:, mine])
    load_m.wait()
    load.wait()
    sum_tiles(c)

    pl.semaphore_wait(barrier, 1 + (CHIPS - 1) + (NZ - 1))

    over_v = send(vs.at[:, theirs], vr, vss, vsr, partner)
    over_v.start()
    over_m = send(mv.at[c], mv.at[c], mss, msr, partner)
    over_m.start()
    over_x = send(x_hbm.at[:, theirs], xh.at[c], xs, xr, partner)
    over_x.start()

    def v_copy(n, d):
        ref = vq.at[n, chip]
        return send(ref, ref, ag_s.at[n, d - 1], ag_r.at[n, d - 1], plane(d))

    def gather_start(n):
        each(CHIPS, lambda d: v_copy(n, d).start())

    gather_start(c)
    over_v.wait_recv()
    put(vq.at[other, chip], vr[...])
    gather_start(other)

    over_m.wait_recv()
    names = pltpu.make_async_copy(mv, smm, nsem)
    names.start()
    names.wait()
    lane = lax.broadcasted_iota(I32, (1, LANES), 1)
    for h in range(2):
        low = jnp.full((1, LANES), BLOCKS, I32)
        high = low
        hits = jnp.zeros((1, LANES), I32)
        for b in range(BLOCKS):
            hit = lane == smm[h, 0, b]
            low = jnp.where(hit & (hits == 0), b, low)
            high = jnp.where(hit & (hits > 0), b, high)
            hits = jnp.where(hit, hits + 1, hits)
        row = jnp.concatenate([mv[h], jnp.zeros((1, LANES - BLOCKS), I32)], axis=1)
        tab[h] = jnp.concatenate([row, low, high, jnp.zeros((5, LANES), I32)], axis=0)
    move = pltpu.make_async_copy(tab, smt, tsem)
    move.start()
    over_x.wait_recv()
    sum_tiles(other)
    move.wait()

    def total(ref, j):
        f0, s0 = smt[0, 1, j], smt[0, 2, j]
        f1, s1 = smt[1, 1, j], smt[1, 2, j]
        return (ref[0, f0] + ref[0, s0]) + (ref[1, f1] + ref[1, s1])

    def node_sums(i, carry):
        for n in range(2):
            snode[i, n] = total(sblk, 2 * i + n)
        return carry

    lax.fori_loop(0, CHIPS, node_sums, 0)
    sr[chip] = snode[chip]

    def ms(d):
        return send(snode.at[chip_at(d)], sr.at[chip], ms_s.at[d - 1], ms_r.at[d - 1], plane(d))

    def mz(d):
        return send(sz.at[z], sz.at[z], mz_s.at[d - 1], mz_r.at[d - 1], column(d))

    def ma(d):
        return send(mm.at[chip], mm.at[chip], ma_s.at[d - 1], ma_r.at[d - 1], plane(d))

    each(CHIPS, lambda d: ms(d).start())

    def sums_to_column():
        each(CHIPS, lambda d: ms(d).wait_recv())
        acc = sr[0]
        for i in range(1, CHIPS):
            acc = acc + sr[i]
        sz[z] = acc
        each(NZ, lambda d: mz(d).start())

    def means_to_plane():
        each(NZ, lambda d: mz(d).wait_recv())
        acc = sz[0]
        for i in range(1, NZ):
            acc = acc + sz[i]
        tile_row = lax.broadcasted_iota(I32, (2, 8, LANES), 1)
        mm[chip] = jnp.where(tile_row < KT, acc / acc[:, KT : KT + 1, :], acc)
        each(CHIPS, lambda d: ma(d).start())
        each(CHIPS, lambda d: ma(d).wait_recv())

    def offsets():
        def body(j, carry):
            dots = None
            for k in range(KT):
                cut = slice(LANES * k, LANES * (k + 1))
                v = vhl[j, 0:DIRS, cut].astype(F32) + vhl[j, DIRS : 2 * DIRS, cut].astype(F32)
                term = v * mm[j // 2, j % 2, k : k + 1, :]
                dots = term if dots is None else dots + term
            shift0[j] = jnp.broadcast_to(jnp.sum(dots, axis=1, keepdims=True), (DIRS, LANES))
            return carry

        lax.fori_loop(0, 32, body, 0)

    over_h = send(shift0, shift1, h_s, h_r, partner)

    def convert(n, i, first):
        ref = vq.at[n, i]
        scale = scale_of(ref)
        his, los, dots = [], [], None
        for k in range(KT):
            q = ref[k].astype(I32)
            hi = ((q >> 8) << 8).astype(F32) * scale
            lo = (q & 255).astype(F32) * scale
            his.append(hi.astype(BF16))
            los.append(lo.astype(BF16))
            if not first:
                term = (hi + lo) * mm[i, n, k : k + 1, :]
                dots = term if dots is None else dots + term
        j = 2 * i + n
        vhl[j, 0:DIRS, :] = jnp.concatenate(his, axis=1)
        vhl[j, DIRS : 2 * DIRS, :] = jnp.concatenate(los, axis=1)
        if first:
            shift[j] = jnp.zeros((DIRS, LANES), F32)
        else:
            shift[j] = jnp.broadcast_to(jnp.sum(dots, axis=1, keepdims=True), (DIRS, LANES))

    def receive(first):
        for n in range(2):
            convert(n, chip, first)

            def arrived(d):
                v_copy(n, d).wait_recv()
                convert(n, chip_from(d), first)

            each(CHIPS, arrived)

    def project(h):
        def one(t):
            at = pl.ds(pl.multiple_of(t * TILE, TILE), TILE)
            parts, shifts = [], []
            for i in range(PER):
                m = smt[h, 0, PER * t + i]
                parts.append(vhl[m])
                shifts.append(shift[m])
            p2 = lax.dot_general(
                jnp.concatenate(parts, axis=0), xh[h, at, :], (((1,), (1,)), ((), ())),
                preferred_element_type=F32,
            )
            out = jnp.zeros((DIRS, TILE), F32)
            for i in range(PER):
                a = 2 * DIRS * i
                p = p2[a : a + DIRS] + p2[a + DIRS : a + 2 * DIRS]
                p = p - jnp.concatenate([shifts[i], shifts[i]], axis=1)
                out = jnp.where(group == i, p, out)
            pc[h, :, at] = out

        def body(t, carry):
            one(2 * t)
            one(2 * t + 1)
            return carry

        lax.fori_loop(0, TILES // 2, body, 0)

    def p_copy(h):
        return send(pc.at[h], pr.at[h], p_s.at[h], p_r.at[h], partner)

    def expand(h):
        def one(t):
            at = pl.ds(pl.multiple_of(t * TILE, TILE), TILE)
            p = pc[h, :, at] + pr[h, :, at]
            hi = p.astype(BF16).astype(F32)
            lo = p - hi
            parts = []
            for i in range(PER):
                parts.append(jnp.where(group == i, hi, 0.0).astype(BF16))
                parts.append(jnp.where(group == i, lo, 0.0).astype(BF16))
            w2 = jnp.dot(jnp.concatenate(parts, axis=0), xh[h, at, :], preferred_element_type=F32)
            for i in range(PER):
                a = 2 * DIRS * i
                wblk[h, PER * t + i] = w2[a : a + DIRS] + w2[a + DIRS : a + 2 * DIRS]

        def body(t, carry):
            one(2 * t)
            one(2 * t + 1)
            return carry

        lax.fori_loop(0, TILES // 2, body, 0)

    def w_copy(n, d):
        return send(
            wq.at[n, chip_at(d)], rq.at[n, chip], rs_s.at[n, d - 1], rs_r.at[n, d - 1], plane(d)
        )

    def z_copy(step, n, d):
        ref = zq.at[step, n, z]
        return send(ref, ref, z_s.at[step, n, d - 1], z_r.at[step, n, d - 1], column(d))

    def g_copy(n):
        return send(gs.at[n], gr.at[n], g_s.at[n], g_r.at[n], partner)

    def node_total(n, i, first):
        j = 2 * i + n
        w = total(wblk, j)
        if first:
            off = shift0[j] + shift1[j]
            w = w - jnp.concatenate([off * snode[i, n, k : k + 1, :] for k in range(KT)], axis=1)
        return w

    def scatter_start(n, first):
        def go(d):
            put(wq.at[n, chip_at(d)], node_total(n, chip_at(d), first))
            w_copy(n, d).start()

        each(CHIPS, go)
        put(rq.at[n, chip], node_total(n, chip, first))

    def term(ref):
        scale = scale_of(ref)
        return tuple(ref[k].astype(I32).astype(F32) * scale for k in range(KT))

    def plane_total(n):
        def body(d, acc):
            w_copy(n, d).wait_recv()
            return tuple(a + b for a, b in zip(acc, term(rq.at[n, chip_from(d)])))

        return jnp.concatenate(lax.fori_loop(1, CHIPS, body, term(rq.at[n, chip])), axis=1)

    def column_total(step, n):
        acc = term(zq.at[step, n, 0])
        for i in range(1, NZ):
            acc = tuple(a + b for a, b in zip(acc, term(zq.at[step, n, i])))
        return jnp.concatenate(acc, axis=1)

    row_id = lax.broadcasted_iota(I32, (DIRS, 1), 0)

    def orthonormal(g, w):
        scale = jnp.zeros((DIRS, 1), F32)
        for k in range(0, DIRS, 2):
            c0, c1 = g[:, k : k + 1], g[:, k + 1 : k + 2]
            p, q, r = c0[k : k + 1], c0[k + 1 : k + 2], c1[k + 1 : k + 2]
            inv = 1.0 / p
            low = q * inv
            pivot = r - q * low
            f1 = (c1 - low * c0) / pivot
            f0 = c0 * inv - low * f1
            below = row_id > k + 1
            f0 = jnp.where(below, f0, jnp.where(row_id == k + 1, low, 0.0))
            f1 = jnp.where(below, f1, 0.0)
            scale = jnp.where(row_id == k, 1.0 / jnp.sqrt(p), scale)
            scale = jnp.where(row_id == k + 1, 1.0 / jnp.sqrt(pivot), scale)
            g = g - f0 * g[k : k + 1, :] - f1 * g[k + 1 : k + 2, :]
            w = w - f0 * w[k : k + 1, :] - f1 * w[k + 1 : k + 2, :]
        return w * scale

    def one_pass(step, first):
        receive(first)
        for h in range(2):
            project(h)
            p_copy(h).start()
        for n in range(2):
            each(CHIPS, lambda d: v_copy(n, d).wait_send())
        if first:
            sums_to_column()
        for h in range(2):
            p_copy(h).wait_recv()
            expand(h)
        if first:
            means_to_plane()
            offsets()
            over_h.start()
            over_h.wait_recv()
        for n in range(2):
            scatter_start(n, first)
        for n in range(2):
            put(zq.at[step, n, z], plane_total(n))
            each(NZ, lambda d: z_copy(step, n, d).start())
        ws = []
        for n in range(2):
            each(NZ, lambda d: z_copy(step, n, d).wait_recv())
            size = mm[chip, n, KT : KT + 1, :]
            w = column_total(step, n) / jnp.concatenate([size] * KT, axis=1)
            ws.append(w)
            gs[n, :, 0:DIRS] = lax.dot_general(
                w, w, (((1,), (1,)), ((), ())), precision=lax.Precision.HIGHEST,
                preferred_element_type=F32,
            )
            g_copy(n).start()
        for n in range(2):
            g_copy(n).wait_recv()
            v = orthonormal(gs[n, :, 0:DIRS] + gr[n, :, 0:DIRS], ws[n])
            vout[n] = v
            put(vq.at[n, chip], v)
            gather_start(n)
        for n in range(2):
            p_copy(n).wait_send()
            g_copy(n).wait_send()
            each(CHIPS, lambda d: w_copy(n, d).wait_send())
            each(NZ, lambda d: z_copy(step, n, d).wait_send())

    one_pass(0, True)

    def later(step, carry):
        one_pass(step, False)
        return carry

    lax.fori_loop(1, PASSES, later, 0)

    over_o = send(vout.at[other], vin, o_s, o_r, partner)
    over_o.start()
    dirs[:, mine] = vout[c]
    receive(False)
    project(other)
    p_copy(other).start()
    project(c)
    over_o.wait_recv()
    dirs[:, theirs] = vin[...]
    back = send(pc.at[other], pr.at[c], p_s.at[other], p_r.at[c], partner)
    back.wait_recv()
    coords[...] = (pc[c] + pr[c]).astype(BF16)
    back.wait_send()
    for cp in (over_o, over_v, over_m, over_x, over_h):
        cp.wait_send()
    for n in range(2):
        each(CHIPS, lambda d: v_copy(n, d).wait_send())
    each(CHIPS, lambda d: ms(d).wait_send())
    each(CHIPS, lambda d: ma(d).wait_send())
    each(NZ, lambda d: mz(d).wait_send())


def on_device(embeddings, membership, start):
    member = membership.reshape(1, BLOCKS)
    vmem = pl.BlockSpec(memory_space=pltpu.VMEM)
    hbm = pl.BlockSpec(memory_space=pltpu.HBM)
    dma = pltpu.SemaphoreType.DMA
    dirs, coords = pl.pallas_call(
        kernel,
        out_shape=(
            jax.ShapeDtypeStruct((DIRS, D), F32),
            jax.ShapeDtypeStruct((DIRS, ROWS), BF16),
        ),
        in_specs=[hbm, hbm, hbm],
        out_specs=(vmem, vmem),
        scratch_shapes=[
            pltpu.VMEM((2, ROWS, HALF), BF16),
            pltpu.SMEM((2, 8, LANES), I32),
            pltpu.SMEM((2, 1, BLOCKS), I32),
            pltpu.VMEM((2, 1, BLOCKS), I32),
            pltpu.VMEM((2, 8, LANES), I32),
            pltpu.VMEM((DIRS, D), F32),
            pltpu.VMEM((DIRS, HALF), F32),
            pltpu.VMEM((2, CHIPS, KT + 1, DIRS, LANES), I16),
            pltpu.VMEM((32, 2 * DIRS, HALF), BF16),
            pltpu.VMEM((32, DIRS, LANES), F32),
            pltpu.VMEM((32, DIRS, LANES), F32),
            pltpu.VMEM((32, DIRS, LANES), F32),
            pltpu.VMEM((2, DIRS, ROWS), F32),
            pltpu.VMEM((2, DIRS, ROWS), F32),
            pltpu.VMEM((2, BLOCKS + 1, DIRS, HALF), F32),
            pltpu.VMEM((2, CHIPS, KT + 1, DIRS, LANES), I16),
            pltpu.VMEM((2, CHIPS, KT + 1, DIRS, LANES), I16),
            pltpu.VMEM((PASSES, 2, NZ, KT + 1, DIRS, LANES), I16),
            pltpu.VMEM((2, DIRS, LANES), F32),
            pltpu.VMEM((2, DIRS, LANES), F32),
            pltpu.VMEM((2, DIRS, HALF), F32),
            pltpu.VMEM((DIRS, HALF), F32),
            pltpu.VMEM((2, BLOCKS + 1, 8, LANES), F32),
            pltpu.VMEM((CHIPS, 2, 8, LANES), F32),
            pltpu.VMEM((CHIPS, 2, 8, LANES), F32),
            pltpu.VMEM((NZ, 2, 8, LANES), F32),
            pltpu.VMEM((CHIPS, 2, 8, LANES), F32),
            dma, dma, dma, dma, dma, dma, dma, dma, dma, dma, dma, dma, dma,
            dma((2, 15)), dma((2, 15)),
            dma((2,)), dma((2,)),
            dma((2, 15)), dma((2, 15)),
            dma((PASSES, 2, 7)), dma((PASSES, 2, 7)),
            dma((2,)), dma((2,)),
            dma((15,)), dma((15,)), dma((7,)), dma((7,)), dma((15,)), dma((15,)),
            dma, dma,
        ],
        compiler_params=pltpu.CompilerParams(
            collective_id=0, has_side_effects=True, vmem_limit_bytes=40 * 1024 * 1024
        ),
    )(member, embeddings, start)
    return (dirs[None], coords)


def solution(mesh):
    return jax.shard_map(
        on_device,
        mesh=mesh,
        in_specs=(P(("node", "rows"), None), P(("node", "rows"), None), P("node", None, None)),
        out_specs=(P("node", None, None), P(None, ("node", "rows"))),
        check_vma=False,
    )
```

```python
import jax
import jax.numpy as jnp
from jax import lax
from jax.experimental import pallas as pl
from jax.experimental.pallas import tpu as pltpu
from jax.sharding import PartitionSpec as P

PASSES = 3
MESH = pl.DeviceIdType.MESH
F32 = jnp.float32
BF16 = jnp.bfloat16
I16 = jnp.int16
I32 = jnp.int32

DIRS = 16
D = 1024
HALF = 512
LANES = 128
KT = HALF // LANES
CHUNK = 256
CT = CHUNK // LANES
ROWS = 2048
BLOCK = 64
BLOCKS = 32
TILE = 256
PER = TILE // BLOCK
TILES = ROWS // TILE
CHIPS = 16
NZ = 8


def lane_half():
    return lax.broadcasted_iota(I32, (DIRS, LANES), 1) < LANES // 2


def put(ref, pair):
    exponents = []
    for n, w in enumerate(pair):
        tiles = [w[:, LANES * k : LANES * (k + 1)] for k in range(CT)]
        top = jnp.maximum(jnp.abs(tiles[0]), jnp.abs(tiles[1]))
        top = jnp.maximum(jnp.max(top, axis=1, keepdims=True), 1e-30)
        e = jnp.floor(jnp.log2(top))
        scale = jnp.exp2(14.0 - e)
        for k in range(CT):
            q = jnp.clip(jnp.round(tiles[k] * scale), -32767.0, 32767.0)
            ref[CT * n + k] = q.astype(I32).astype(I16)
        exponents.append(jnp.broadcast_to(e.astype(I32), (DIRS, LANES)))
    ref[2 * CT] = jnp.where(lane_half(), exponents[0], exponents[1]).astype(I16)


def scales_of(ref):
    s = jnp.exp2(ref[2 * CT].astype(I32).astype(F32) - 14.0)
    return [jnp.broadcast_to(s[:, LANES // 2 * n : LANES // 2 * n + 1], (DIRS, LANES)) for n in range(2)]


def kernel(
    member, x_hbm, start, dirs, coords,
    xh, smt, smm, mv, tab, vs, vr, vq, vhl, shift, shift0, shift1, pc, pr, pst, wblk, wq, rq, zq, gs, gr, vout, vin,
    sblk, snode, sr, sz, mm, ds, dr,
    xsem, xs, xr, msem, mss, msr, nsem, tsem, vsem, vss, vsr, h_s, h_r, ag_s, ag_r, p_s, p_r, rs_s, rs_r, z_s, z_r, g_s, g_r,
    ms_s, ms_r, mz_s, mz_r, ma_s, ma_r, d_s, d_r, o_s, o_r,
):
    me = lax.axis_index("node")
    z = lax.axis_index("rows")
    x, y, c = me >> 3, (me >> 1) & 3, me & 1
    chip = me >> 1
    other = 1 - c

    def chip_at(d):
        return (((x + (d >> 2)) & 3) << 2) + ((y + d) & 3)

    def chip_from(d):
        return (((x + 4 - (d >> 2)) & 3) << 2) + ((y + 4 - (d & 3)) & 3)

    def plane(d):
        return (chip_at(d) * 2 + c, z)

    def column(d):
        return (me, (z + d) & (NZ - 1))

    partner = (chip * 2 + other, z)

    def send(src, dst, ssem, rsem, to):
        return pltpu.make_async_remote_copy(
            src_ref=src, dst_ref=dst, send_sem=ssem, recv_sem=rsem, device_id=to, device_id_type=MESH
        )

    def each(n, what):
        if n == NZ:
            for d in range(1, NZ):
                what(d)
        else:
            grouped(lambda ds: [what(d) for d in ds])

    def grouped(what, carry=0):
        def body(g, carry):
            ds = [5 * g + r for r in range(1, 6)]
            if carry_used:
                return what(ds, carry)
            what(ds)
            return carry

        carry_used = not isinstance(carry, int)
        return lax.fori_loop(0, 3, body, carry)

    mine = pl.ds(pl.multiple_of(c * HALF, HALF), HALF)
    theirs = pl.ds(pl.multiple_of(other * HALF, HALF), HALF)
    load = pltpu.make_async_copy(x_hbm.at[:, mine], xh.at[c], xsem)
    load.start()
    load_m = pltpu.make_async_copy(member, mv.at[c], msem)
    load_m.start()
    load_v = pltpu.make_async_copy(start.at[0], vs, vsem)
    load_v.start()

    barrier = pltpu.get_barrier_semaphore()
    pl.semaphore_signal(barrier, inc=1, device_id=partner, device_id_type=MESH)

    def greet_plane(d):
        pl.semaphore_signal(barrier, inc=1, device_id=plane(d), device_id_type=MESH)

    def greet_column(d):
        pl.semaphore_signal(barrier, inc=1, device_id=column(d), device_id_type=MESH)

    each(CHIPS, greet_plane)
    each(NZ, greet_column)

    group = lax.broadcasted_iota(I32, (DIRS, TILE), 1) >> 6
    ones_rows = (lax.broadcasted_iota(I32, (DIRS, TILE), 0) == group).astype(F32).astype(BF16)

    def sum_tiles(h):
        def body(t, carry):
            tile = xh[h, pl.ds(pl.multiple_of(t * TILE, TILE), TILE), :]
            s = jnp.dot(ones_rows, tile, preferred_element_type=F32)
            for i in range(PER):
                rows = [s[i : i + 1, LANES * k : LANES * (k + 1)] for k in range(KT)]
                rows.append(jnp.full((1, LANES), float(BLOCK), F32))
                rows.append(jnp.zeros((3, LANES), F32))
                sblk[h, PER * t + i] = jnp.concatenate(rows, axis=0)
            return carry

        lax.fori_loop(0, TILES, body, 0)

    wblk[0, BLOCKS] = jnp.zeros((DIRS, HALF), F32)
    wblk[1, BLOCKS] = jnp.zeros((DIRS, HALF), F32)
    sblk[0, BLOCKS] = jnp.zeros((8, LANES), F32)
    sblk[1, BLOCKS] = jnp.zeros((8, LANES), F32)
    load_v.wait()
    load_m.wait()
    load.wait()
    sum_tiles(c)

    pl.semaphore_wait(barrier, 1 + (CHIPS - 1) + (NZ - 1))

    over_v = send(vs.at[:, theirs], vr, vss, vsr, partner)
    over_v.start()
    over_m = send(mv.at[c], mv.at[c], mss, msr, partner)
    over_m.start()
    over_x = send(x_hbm.at[:, theirs], xh.at[c], xs, xr, partner)
    over_x.start()

    def v_copy(n, d):
        ref = vq.at[n, chip]
        return send(ref, ref, ag_s.at[n, d - 1], ag_r.at[n, d - 1], plane(d))

    def gather_start(n):
        each(CHIPS, lambda d: v_copy(n, d).start())

    over_v.wait_recv()
    own, pair = vs[:, mine], vr[...]
    for q in range(2):
        at = slice(CHUNK * q, CHUNK * (q + 1))
        put(
            vq.at[q, chip],
            [jnp.where(c == 0, own[:, at], pair[:, at]), jnp.where(c == 0, pair[:, at], own[:, at])],
        )
        gather_start(q)

    over_m.wait_recv()
    names = pltpu.make_async_copy(mv, smm, nsem)
    names.start()
    names.wait()
    lane = lax.broadcasted_iota(I32, (1, LANES), 1)
    for h in range(2):
        low = jnp.full((1, LANES), BLOCKS, I32)
        high = low
        hits = jnp.zeros((1, LANES), I32)
        for b in range(BLOCKS):
            hit = lane == smm[h, 0, b]
            low = jnp.where(hit & (hits == 0), b, low)
            high = jnp.where(hit & (hits > 0), b, high)
            hits = jnp.where(hit, hits + 1, hits)
        row = jnp.concatenate([mv[h], jnp.zeros((1, LANES - BLOCKS), I32)], axis=1)
        tab[h] = jnp.concatenate([row, low, high, jnp.zeros((5, LANES), I32)], axis=0)
    move = pltpu.make_async_copy(tab, smt, tsem)
    move.start()
    over_x.wait_recv()
    sum_tiles(other)
    move.wait()

    def total(ref, j):
        f0, s0 = smt[0, 1, j], smt[0, 2, j]
        f1, s1 = smt[1, 1, j], smt[1, 2, j]
        return (ref[0, f0] + ref[0, s0]) + (ref[1, f1] + ref[1, s1])

    def node_sums(i, carry):
        for n in range(2):
            snode[i, n] = total(sblk, 2 * i + n)
        return carry

    lax.fori_loop(0, CHIPS, node_sums, 0)
    sr[chip] = snode[chip]

    def ms(d):
        return send(snode.at[chip_at(d)], sr.at[chip], ms_s.at[d - 1], ms_r.at[d - 1], plane(d))

    def mz(d):
        return send(sz.at[z], sz.at[z], mz_s.at[d - 1], mz_r.at[d - 1], column(d))

    def ma(d):
        return send(mm.at[chip], mm.at[chip], ma_s.at[d - 1], ma_r.at[d - 1], plane(d))

    each(CHIPS, lambda d: ms(d).start())

    tile_row = lax.broadcasted_iota(I32, (2, 8, LANES), 1)

    def means(a):
        return jnp.where(tile_row < KT, a / jnp.maximum(a[:, KT : KT + 1, :], 1.0), a)

    def plane_sums():
        each(CHIPS, lambda d: ms(d).wait_recv())
        acc = sr[0]
        for i in range(1, CHIPS):
            acc = acc + sr[i]
        sz[z] = acc
        each(NZ, lambda d: mz(d).start())

    def dots(v, a, n):
        out = None
        for k in range(KT):
            part = v[:, LANES * k : LANES * (k + 1)] * a[n, k : k + 1, :]
            out = part if out is None else out + part
        return jnp.sum(out, axis=1, keepdims=True)

    def vector_of(j):
        return vhl[j, 0:DIRS, :].astype(F32) + vhl[j, DIRS : 2 * DIRS, :].astype(F32)

    def offsets():
        def body(g, carry):
            for i in (4 * g, 4 * g + 1, 4 * g + 2, 4 * g + 3):
                a = means(snode[i])
                for n in range(2):
                    shift0[2 * i + n] = jnp.broadcast_to(dots(vector_of(2 * i + n), a, n), (DIRS, LANES))
            return carry

        lax.fori_loop(0, CHIPS // 4, body, 0)

    over_h = send(shift0, shift1, h_s, h_r, partner)
    over_d = send(ds, dr, d_s, d_r, partner)

    def scatter_of(d, first_lane, parts, whole, n):
        count = [part[n, KT : KT + 1, 0:1] for part in parts]
        centre = jnp.zeros((DIRS, 1), F32)
        for i, t in enumerate(count):
            centre = centre + d[:, first_lane + i : first_lane + i + 1] * t
        centre = centre / jnp.maximum(whole[n, KT : KT + 1, 0:1], 1.0)
        m = means(whole)
        out = [jnp.zeros((DIRS, LANES), F32) for _ in range(KT)]
        for i, t in enumerate(count):
            a = means(parts[i])
            weight = (d[:, first_lane + i : first_lane + i + 1] - centre) * t
            for k in range(KT):
                out[k] = out[k] + weight * (a[n, k : k + 1, :] - m[n, k : k + 1, :])
        return jnp.concatenate(out, axis=1)

    def between():
        each(NZ, lambda d: mz(d).wait_recv())
        chips = [sr[i] for i in range(CHIPS)]
        planes = [sz[i] for i in range(NZ)]
        every = planes[0]
        for i in range(1, NZ):
            every = every + planes[i]
        mm[chip] = means(every)
        each(CHIPS, lambda d: ma(d).start())
        lanes = lax.broadcasted_iota(I32, (DIRS, LANES), 1)
        for n in range(2):
            v = vector_of(2 * chip + n)
            out = jnp.zeros((DIRS, LANES), F32)
            for i, part in enumerate(chips + planes):
                out = jnp.where(lanes == i, dots(v, means(part), n), out)
            ds[n] = out
        over_d.start()
        over_d.wait_recv()
        both = [ds[n] + dr[n] for n in range(2)]
        inner = [scatter_of(both[n], 0, chips, sz[z], n) for n in range(2)]
        outer = [scatter_of(both[n], CHIPS, planes, every, n) for n in range(2)]
        return inner, outer

    def convert(q, i, first):
        ref = vq.at[q, i]
        scales = scales_of(ref)
        for n in range(2):
            j = 2 * i + n
            his, los, dots = [], [], None
            for k in range(CT):
                v = ref[CT * n + k].astype(I32)
                hi = ((v >> 8) << 8).astype(F32) * scales[n]
                lo = (v & 255).astype(F32) * scales[n]
                his.append(hi.astype(BF16))
                los.append(lo.astype(BF16))
                if not first:
                    part = (hi + lo) * mm[i, n, CT * q + k : CT * q + k + 1, :]
                    dots = part if dots is None else dots + part
            at = slice(CHUNK * q, CHUNK * (q + 1))
            vhl[j, 0:DIRS, at] = jnp.concatenate(his, axis=1)
            vhl[j, DIRS : 2 * DIRS, at] = jnp.concatenate(los, axis=1)
            if not first:
                dots = jnp.broadcast_to(jnp.sum(dots, axis=1, keepdims=True), (DIRS, LANES))
                shift[j] = dots if q == 0 else shift[j] + dots

    def receive(q, first):
        convert(q, chip, first)

        def arrived(ds):
            for d in ds:
                v_copy(q, d).wait_recv()
            for d in ds:
                convert(q, chip_from(d), first)

        grouped(arrived)

    def project(q, h, first):
        cols = slice(CHUNK * q, CHUNK * (q + 1))

        def one(t):
            at = pl.ds(pl.multiple_of(t * TILE, TILE), TILE)
            parts, shifts = [], []
            for i in range(PER):
                m = smt[h, 0, PER * t + i]
                parts.append(vhl[m, :, cols])
                if q == 1 and not first:
                    shifts.append(shift[m])
            p2 = lax.dot_general(
                jnp.concatenate(parts, axis=0), xh[h, at, cols], (((1,), (1,)), ((), ())),
                preferred_element_type=F32,
            )
            out = jnp.zeros((DIRS, TILE), F32)
            for i in range(PER):
                a = 2 * DIRS * i
                p = p2[a : a + DIRS] + p2[a + DIRS : a + 2 * DIRS]
                if q == 1 and not first:
                    p = p - jnp.concatenate([shifts[i], shifts[i]], axis=1)
                out = jnp.where(group == i, p, out)
            pc[h, :, at] = out if q == 0 else pc[h, :, at] + out

        def body(t, carry):
            one(2 * t)
            one(2 * t + 1)
            return carry

        lax.fori_loop(0, TILES // 2, body, 0)

    def p_copy(h):
        return send(pc.at[h], pr.at[h], p_s.at[h], p_r.at[h], partner)

    def expand(q, h):
        cols = slice(CHUNK * q, CHUNK * (q + 1))

        def one(t):
            at = pl.ds(pl.multiple_of(t * TILE, TILE), TILE)
            if q == 0:
                p = pc[h, :, at] + pr[h, :, at]
                hi = p.astype(BF16).astype(F32)
                lo = p - hi
                parts = []
                for i in range(PER):
                    parts.append(jnp.where(group == i, hi, 0.0).astype(BF16))
                    parts.append(jnp.where(group == i, lo, 0.0).astype(BF16))
                stack = jnp.concatenate(parts, axis=0)
                pst[h, t] = stack
            else:
                stack = pst[h, t]
            w2 = jnp.dot(stack, xh[h, at, cols], preferred_element_type=F32)
            for i in range(PER):
                a = 2 * DIRS * i
                wblk[h, PER * t + i, :, cols] = w2[a : a + DIRS] + w2[a + DIRS : a + 2 * DIRS]

        def body(t, carry):
            one(2 * t)
            one(2 * t + 1)
            return carry

        lax.fori_loop(0, TILES // 2, body, 0)

    def w_copy(n, d):
        return send(
            wq.at[n, chip_at(d)], rq.at[n, chip], rs_s.at[n, d - 1], rs_r.at[n, d - 1], plane(d)
        )

    def z_copy(step, n, d):
        ref = zq.at[step, n, z]
        return send(ref, ref, z_s.at[step, n, d - 1], z_r.at[step, n, d - 1], column(d))

    g_copy = send(gs, gr, g_s, g_r, partner)

    def total_of(j, cols):
        f0, s0 = smt[0, 1, j], smt[0, 2, j]
        f1, s1 = smt[1, 1, j], smt[1, 2, j]
        return (wblk[0, f0, :, cols] + wblk[0, s0, :, cols]) + (
            wblk[1, f1, :, cols] + wblk[1, s1, :, cols]
        )

    def node_totals(q, i, first):
        out = []
        for n in range(2):
            j = 2 * i + n
            w = total_of(j, slice(CHUNK * q, CHUNK * (q + 1)))
            if first:
                off = shift0[j] + shift1[j]
                rows = [snode[i, n, CT * q + k : CT * q + k + 1, :] for k in range(CT)]
                w = w - jnp.concatenate([off * r for r in rows], axis=1)
            out.append(w)
        return out

    def scatter_start(q, first):
        def go(ds):
            for d in ds:
                put(wq.at[q, chip_at(d)], node_totals(q, chip_at(d), first))
            for d in ds:
                w_copy(q, d).start()

        grouped(go)
        put(rq.at[q, chip], node_totals(q, chip, first))

    def term(ref):
        scales = scales_of(ref)
        return tuple(ref[k].astype(I32).astype(F32) * scales[k // CT] for k in range(2 * CT))

    def paired(acc):
        return [jnp.concatenate(acc[CT * n : CT * (n + 1)], axis=1) for n in range(2)]

    def plane_total(q):
        def body(ds, acc):
            for d in ds:
                w_copy(q, d).wait_recv()
            for d in ds:
                acc = tuple(a + b for a, b in zip(acc, term(rq.at[q, chip_from(d)])))
            return acc

        return paired(grouped(body, term(rq.at[q, chip])))

    def column_total(step, q):
        acc = term(zq.at[step, q, 0])
        for i in range(1, NZ):
            acc = tuple(a + b for a, b in zip(acc, term(zq.at[step, q, i])))
        return paired(acc)

    row_id = lax.broadcasted_iota(I32, (DIRS, 1), 0)

    def orthonormal(gw):
        scales = [jnp.zeros((DIRS, 1), F32)] * 2
        for k in range(0, DIRS, 2):
            for n in range(2):
                (g, w), scale = gw[n], scales[n]
                c0, c1 = g[:, k : k + 1], g[:, k + 1 : k + 2]
                p, q, r = c0[k : k + 1], c0[k + 1 : k + 2], c1[k + 1 : k + 2]
                inv = 1.0 / p
                low = q * inv
                pivot = r - q * low
                f1 = (c1 - low * c0) / pivot
                f0 = c0 * inv - low * f1
                below = row_id > k + 1
                f0 = jnp.where(below, f0, jnp.where(row_id == k + 1, low, 0.0))
                f1 = jnp.where(below, f1, 0.0)
                scale = jnp.where(row_id == k, 1.0 / jnp.sqrt(p), scale)
                scales[n] = jnp.where(row_id == k + 1, 1.0 / jnp.sqrt(pivot), scale)
                g = g - f0 * g[k : k + 1, :] - f1 * g[k + 1 : k + 2, :]
                w = w - f0 * w[k : k + 1, :] - f1 * w[k + 1 : k + 2, :]
                gw[n] = (g, w)
        return [gw[n][1] * scales[n] for n in range(2)]

    def one_pass(step, first):
        for q in range(2):
            receive(q, first)
            if first and q == 1:
                offsets()
                over_h.start()
            for h in range(2):
                project(q, h, first)
                if q == 1:
                    p_copy(h).start()
            if first and q == 0:
                plane_sums()
        for q in range(2):
            each(CHIPS, lambda d: v_copy(q, d).wait_send())
        for h in range(2):
            p_copy(h).wait_recv()
            expand(0, h)
        if first:
            over_h.wait_recv()
        scatter_start(0, first)
        for h in range(2):
            expand(1, h)
        scatter_start(1, first)
        if first:
            inner, outer = between()
        for q in range(2):
            total = plane_total(q)
            if first:
                total = [total[n] + inner[n][:, CHUNK * q : CHUNK * (q + 1)] for n in range(2)]
            put(zq.at[step, q, z], total)
            each(NZ, lambda d: z_copy(step, q, d).start())
        halves = []
        for q in range(2):
            each(NZ, lambda d: z_copy(step, q, d).wait_recv())
            halves.append(column_total(step, q))
        ws = []
        for n in range(2):
            w = jnp.concatenate([halves[0][n], halves[1][n]], axis=1)
            if first:
                w = w + outer[n]
            w = w / jnp.concatenate([mm[chip, n, KT : KT + 1, :]] * KT, axis=1)
            ws.append(w)
            gs[n, :, 0:DIRS] = lax.dot_general(
                w, w, (((1,), (1,)), ((), ())), precision=lax.Precision.HIGHEST,
                preferred_element_type=F32,
            )
        g_copy.start()
        g_copy.wait_recv()
        vectors = orthonormal([(gs[n, :, 0:DIRS] + gr[n, :, 0:DIRS], ws[n]) for n in range(2)])
        for q in range(2):
            put(vq.at[q, chip], [v[:, CHUNK * q : CHUNK * (q + 1)] for v in vectors])
            gather_start(q)
        for n in range(2):
            vout[n] = vectors[n]
        if first:
            each(CHIPS, lambda d: ma(d).wait_recv())
        g_copy.wait_send()
        for n in range(2):
            p_copy(n).wait_send()
            each(CHIPS, lambda d: w_copy(n, d).wait_send())
            each(NZ, lambda d: z_copy(step, n, d).wait_send())

    one_pass(0, True)

    def later(step, carry):
        one_pass(step, False)
        return carry

    lax.fori_loop(1, PASSES, later, 0)

    over_o = send(vout.at[other], vin, o_s, o_r, partner)
    over_o.start()
    dirs[:, mine] = vout[c]
    for q in range(2):
        receive(q, False)
        project(q, other, False)
        if q == 1:
            p_copy(other).start()
        project(q, c, False)
    over_o.wait_recv()
    dirs[:, theirs] = vin[...]
    back = send(pc.at[other], pr.at[c], p_s.at[other], p_r.at[c], partner)
    back.wait_recv()
    coords[...] = (pc[c] + pr[c]).astype(BF16)
    back.wait_send()
    for cp in (over_o, over_v, over_m, over_x, over_h, over_d):
        cp.wait_send()
    for n in range(2):
        each(CHIPS, lambda d: v_copy(n, d).wait_send())
    each(CHIPS, lambda d: ms(d).wait_send())
    each(CHIPS, lambda d: ma(d).wait_send())
    each(NZ, lambda d: mz(d).wait_send())


def on_device(embeddings, membership, start):
    member = membership.reshape(1, BLOCKS)
    vmem = pl.BlockSpec(memory_space=pltpu.VMEM)
    hbm = pl.BlockSpec(memory_space=pltpu.HBM)
    dma = pltpu.SemaphoreType.DMA
    dirs, coords = pl.pallas_call(
        kernel,
        out_shape=(
            jax.ShapeDtypeStruct((DIRS, D), F32),
            jax.ShapeDtypeStruct((DIRS, ROWS), BF16),
        ),
        in_specs=[hbm, hbm, hbm],
        out_specs=(vmem, vmem),
        scratch_shapes=[
            pltpu.VMEM((2, ROWS, HALF), BF16),
            pltpu.SMEM((2, 8, LANES), I32),
            pltpu.SMEM((2, 1, BLOCKS), I32),
            pltpu.VMEM((2, 1, BLOCKS), I32),
            pltpu.VMEM((2, 8, LANES), I32),
            pltpu.VMEM((DIRS, D), F32),
            pltpu.VMEM((DIRS, HALF), F32),
            pltpu.VMEM((2, CHIPS, KT + 1, DIRS, LANES), I16),
            pltpu.VMEM((32, 2 * DIRS, HALF), BF16),
            pltpu.VMEM((32, DIRS, LANES), F32),
            pltpu.VMEM((32, DIRS, LANES), F32),
            pltpu.VMEM((32, DIRS, LANES), F32),
            pltpu.VMEM((2, DIRS, ROWS), F32),
            pltpu.VMEM((2, DIRS, ROWS), F32),
            pltpu.VMEM((2, TILES, 2 * DIRS * PER, TILE), BF16),
            pltpu.VMEM((2, BLOCKS + 1, DIRS, HALF), F32),
            pltpu.VMEM((2, CHIPS, KT + 1, DIRS, LANES), I16),
            pltpu.VMEM((2, CHIPS, KT + 1, DIRS, LANES), I16),
            pltpu.VMEM((PASSES, 2, NZ, KT + 1, DIRS, LANES), I16),
            pltpu.VMEM((2, DIRS, LANES), F32),
            pltpu.VMEM((2, DIRS, LANES), F32),
            pltpu.VMEM((2, DIRS, HALF), F32),
            pltpu.VMEM((DIRS, HALF), F32),
            pltpu.VMEM((2, BLOCKS + 1, 8, LANES), F32),
            pltpu.VMEM((CHIPS, 2, 8, LANES), F32),
            pltpu.VMEM((CHIPS, 2, 8, LANES), F32),
            pltpu.VMEM((NZ, 2, 8, LANES), F32),
            pltpu.VMEM((CHIPS, 2, 8, LANES), F32),
            pltpu.VMEM((2, DIRS, LANES), F32),
            pltpu.VMEM((2, DIRS, LANES), F32),
            dma, dma, dma, dma, dma, dma, dma, dma, dma, dma, dma, dma, dma,
            dma((2, 15)), dma((2, 15)),
            dma((2,)), dma((2,)),
            dma((2, 15)), dma((2, 15)),
            dma((PASSES, 2, 7)), dma((PASSES, 2, 7)),
            dma, dma,
            dma((15,)), dma((15,)), dma((7,)), dma((7,)), dma((15,)), dma((15,)),
            dma, dma, dma, dma,
        ],
        compiler_params=pltpu.CompilerParams(
            collective_id=0, has_side_effects=True, vmem_limit_bytes=52 * 1024 * 1024
        ),
    )(member, embeddings, start)
    return (dirs[None], coords)


def solution(mesh):
    return jax.shard_map(
        on_device,
        mesh=mesh,
        in_specs=(P(("node", "rows"), None), P(("node", "rows"), None), P("node", None, None)),
        out_specs=(P("node", None, None), P(None, ("node", "rows"))),
        check_vma=False,
    )
```

```python
import jax
import jax.numpy as jnp
from jax import lax
from jax.experimental import pallas as pl
from jax.experimental.pallas import tpu as pltpu
from jax.sharding import PartitionSpec as P

PASSES = 3
MESH = pl.DeviceIdType.MESH
F32 = jnp.float32
BF16 = jnp.bfloat16
I16 = jnp.int16
I32 = jnp.int32

DIRS = 16
D = 1024
HALF = 512
LANES = 128
KT = HALF // LANES
CHUNK = 256
CT = CHUNK // LANES
ROWS = 2048
BLOCK = 64
BLOCKS = 32
TILE = 256
PER = TILE // BLOCK
TILES = ROWS // TILE
CHIPS = 16
NZ = 8
FAR_FIRST = (10, 6, 9, 11, 14, 5, 7, 13, 15, 2, 8, 1, 3, 4, 12)


def lane_half():
    return lax.broadcasted_iota(I32, (DIRS, LANES), 1) < LANES // 2


def put(ref, pair):
    exponents = []
    for n, w in enumerate(pair):
        tiles = [w[:, LANES * k : LANES * (k + 1)] for k in range(CT)]
        top = jnp.maximum(jnp.abs(tiles[0]), jnp.abs(tiles[1]))
        top = jnp.maximum(jnp.max(top, axis=1, keepdims=True), 1e-30)
        e = jnp.floor(jnp.log2(top))
        scale = jnp.exp2(14.0 - e)
        for k in range(CT):
            q = jnp.clip(jnp.round(tiles[k] * scale), -32767.0, 32767.0)
            ref[CT * n + k] = q.astype(I32).astype(I16)
        exponents.append(jnp.broadcast_to(e.astype(I32), (DIRS, LANES)))
    ref[2 * CT] = jnp.where(lane_half(), exponents[0], exponents[1]).astype(I16)


def put_whole(ref, chip, pair):
    exponents = []
    for n, w in enumerate(pair):
        tiles = [w[:, LANES * k : LANES * (k + 1)] for k in range(KT)]
        top = jnp.maximum(
            jnp.maximum(jnp.abs(tiles[0]), jnp.abs(tiles[1])),
            jnp.maximum(jnp.abs(tiles[2]), jnp.abs(tiles[3])),
        )
        top = jnp.maximum(jnp.max(top, axis=1, keepdims=True), 1e-30)
        e = jnp.floor(jnp.log2(top))
        scale = jnp.exp2(14.0 - e)
        for k in range(KT):
            q = jnp.clip(jnp.round(tiles[k] * scale), -32767.0, 32767.0)
            ref[k // CT, chip, CT * n + k % CT] = q.astype(I32).astype(I16)
        exponents.append(jnp.broadcast_to(e.astype(I32), (DIRS, LANES)))
    ref[0, chip, 2 * CT] = jnp.where(lane_half(), exponents[0], exponents[1]).astype(I16)


def scales_of(ref):
    s = jnp.exp2(ref[2 * CT].astype(I32).astype(F32) - 14.0)
    return [jnp.broadcast_to(s[:, LANES // 2 * n : LANES // 2 * n + 1], (DIRS, LANES)) for n in range(2)]


def kernel(
    member, x_hbm, start, dirs, coords,
    xh, smt, smm, mv, tab, vs, vr, vq, vhl, shift, shift0, shift1, pc, pr, pst, wblk, wq, rq, zq, gs, gr, vout, vin,
    sblk, snode, sr, sz, mm, ds, dr,
    xsem, xs, xr, msem, mss, msr, nsem, tsem, vsem, vss, vsr, h_s, h_r, ag_s, ag_r, p_s, p_r, rs_s, rs_r, z_s, z_r, g_s, g_r,
    ms_s, ms_r, mz_s, mz_r, ma_s, ma_r, d_s, d_r, o_s, o_r,
):
    me = lax.axis_index("node")
    z = lax.axis_index("rows")
    x, y, c = me >> 3, (me >> 1) & 3, me & 1
    chip = me >> 1
    other = 1 - c

    def chip_at(d):
        return (((x + (d >> 2)) & 3) << 2) + ((y + d) & 3)

    def chip_from(d):
        return (((x + 4 - (d >> 2)) & 3) << 2) + ((y + 4 - (d & 3)) & 3)

    def plane(d):
        return (chip_at(d) * 2 + c, z)

    def column(d):
        return (me, (z + d) & (NZ - 1))

    partner = (chip * 2 + other, z)

    def send(src, dst, ssem, rsem, to):
        return pltpu.make_async_remote_copy(
            src_ref=src, dst_ref=dst, send_sem=ssem, recv_sem=rsem, device_id=to, device_id_type=MESH
        )

    def each(n, what):
        if n == NZ:
            for d in range(1, NZ):
                what(d)
        else:
            grouped(lambda ds: [what(d) for d in ds])

    def grouped(what, carry=0):
        def body(g, carry):
            ds = [
                jnp.where(g == 0, FAR_FIRST[r], jnp.where(g == 1, FAR_FIRST[r + 5], FAR_FIRST[r + 10]))
                for r in range(5)
            ]
            if carry_used:
                return what(ds, carry)
            what(ds)
            return carry

        carry_used = not isinstance(carry, int)
        return lax.fori_loop(0, 3, body, carry)

    mine = pl.ds(pl.multiple_of(c * HALF, HALF), HALF)
    theirs = pl.ds(pl.multiple_of(other * HALF, HALF), HALF)
    load = pltpu.make_async_copy(x_hbm.at[:, mine], xh.at[c], xsem)
    load.start()
    load_m = pltpu.make_async_copy(member, mv.at[c], msem)
    load_m.start()
    load_v = pltpu.make_async_copy(start.at[0], vs, vsem)
    load_v.start()

    barrier = pltpu.get_barrier_semaphore()
    pl.semaphore_signal(barrier, inc=1, device_id=partner, device_id_type=MESH)

    def greet_plane(d):
        pl.semaphore_signal(barrier, inc=1, device_id=plane(d), device_id_type=MESH)

    def greet_column(d):
        pl.semaphore_signal(barrier, inc=1, device_id=column(d), device_id_type=MESH)

    each(CHIPS, greet_plane)
    each(NZ, greet_column)

    group = lax.broadcasted_iota(I32, (DIRS, TILE), 1) >> 6
    ones_rows = (lax.broadcasted_iota(I32, (DIRS, TILE), 0) == group).astype(F32).astype(BF16)

    def sum_tiles(h):
        def body(t, carry):
            tile = xh[h, pl.ds(pl.multiple_of(t * TILE, TILE), TILE), :]
            s = jnp.dot(ones_rows, tile, preferred_element_type=F32)
            for i in range(PER):
                rows = [s[i : i + 1, LANES * k : LANES * (k + 1)] for k in range(KT)]
                rows.append(jnp.full((1, LANES), float(BLOCK), F32))
                rows.append(jnp.zeros((3, LANES), F32))
                sblk[h, PER * t + i] = jnp.concatenate(rows, axis=0)
            return carry

        lax.fori_loop(0, TILES, body, 0)

    wblk[0, BLOCKS] = jnp.zeros((DIRS, HALF), F32)
    wblk[1, BLOCKS] = jnp.zeros((DIRS, HALF), F32)
    sblk[0, BLOCKS] = jnp.zeros((8, LANES), F32)
    sblk[1, BLOCKS] = jnp.zeros((8, LANES), F32)
    load_v.wait()
    load_m.wait()

    pl.semaphore_wait(barrier, 1 + (CHIPS - 1) + (NZ - 1))

    over_v = send(vs.at[:, theirs], vr, vss, vsr, partner)
    over_v.start()
    over_m = send(mv.at[c], mv.at[c], mss, msr, partner)
    over_m.start()
    over_x = send(x_hbm.at[:, theirs], xh.at[c], xs, xr, partner)
    over_x.start()

    def v_copy(n, d):
        ref = vq.at[n, chip] if n == 0 else vq.at[n, chip, pl.ds(0, 2 * CT)]
        return send(ref, ref, ag_s.at[n, d - 1], ag_r.at[n, d - 1], plane(d))

    def gather_start(n):
        each(CHIPS, lambda d: v_copy(n, d).start())

    over_v.wait_recv()
    own, pair = vs[:, mine], vr[...]
    put_whole(vq, chip, [jnp.where(c == 0, own, pair), jnp.where(c == 0, pair, own)])
    for q in range(2):
        gather_start(q)

    load.wait()
    sum_tiles(c)
    over_m.wait_recv()
    names = pltpu.make_async_copy(mv, smm, nsem)
    names.start()
    names.wait()
    lane = lax.broadcasted_iota(I32, (1, LANES), 1)
    for h in range(2):
        low = jnp.full((1, LANES), BLOCKS, I32)
        high = low
        hits = jnp.zeros((1, LANES), I32)
        for b in range(BLOCKS):
            hit = lane == smm[h, 0, b]
            low = jnp.where(hit & (hits == 0), b, low)
            high = jnp.where(hit & (hits > 0), b, high)
            hits = jnp.where(hit, hits + 1, hits)
        row = jnp.concatenate([mv[h], jnp.zeros((1, LANES - BLOCKS), I32)], axis=1)
        tab[h] = jnp.concatenate([row, low, high, jnp.zeros((5, LANES), I32)], axis=0)
    move = pltpu.make_async_copy(tab, smt, tsem)
    move.start()
    over_x.wait_recv()
    sum_tiles(other)
    move.wait()

    def total(ref, j):
        f0, s0 = smt[0, 1, j], smt[0, 2, j]
        f1, s1 = smt[1, 1, j], smt[1, 2, j]
        return (ref[0, f0] + ref[0, s0]) + (ref[1, f1] + ref[1, s1])

    def node_sums(i, carry):
        for n in range(2):
            snode[i, n] = total(sblk, 2 * i + n)
        return carry

    lax.fori_loop(0, CHIPS, node_sums, 0)
    sr[chip] = snode[chip]

    def ms(d):
        return send(snode.at[chip_at(d)], sr.at[chip], ms_s.at[d - 1], ms_r.at[d - 1], plane(d))

    def mz(d):
        return send(sz.at[z], sz.at[z], mz_s.at[d - 1], mz_r.at[d - 1], column(d))

    def ma(d):
        return send(mm.at[chip], mm.at[chip], ma_s.at[d - 1], ma_r.at[d - 1], plane(d))

    each(CHIPS, lambda d: ms(d).start())

    tile_row = lax.broadcasted_iota(I32, (2, 8, LANES), 1)

    def means(a):
        return jnp.where(tile_row < KT, a / jnp.maximum(a[:, KT : KT + 1, :], 1.0), a)

    def plane_sums():
        each(CHIPS, lambda d: ms(d).wait_recv())
        acc = sr[0]
        for i in range(1, CHIPS):
            acc = acc + sr[i]
        sz[z] = acc
        each(NZ, lambda d: mz(d).start())

    def dots(v, a, n):
        out = None
        for k in range(KT):
            part = v[:, LANES * k : LANES * (k + 1)] * a[n, k : k + 1, :]
            out = part if out is None else out + part
        return jnp.sum(out, axis=1, keepdims=True)

    def vector_of(j):
        return vhl[j, 0:DIRS, :].astype(F32) + vhl[j, DIRS : 2 * DIRS, :].astype(F32)

    def offsets():
        def body(g, carry):
            for i in (4 * g, 4 * g + 1, 4 * g + 2, 4 * g + 3):
                a = means(snode[i])
                for n in range(2):
                    shift0[2 * i + n] = jnp.broadcast_to(dots(vector_of(2 * i + n), a, n), (DIRS, LANES))
            return carry

        lax.fori_loop(0, CHIPS // 4, body, 0)

    over_h = send(shift0, shift1, h_s, h_r, partner)
    over_d = send(ds, dr, d_s, d_r, partner)

    def scatter_of(d, first_lane, parts, whole, n):
        count = [part[n, KT : KT + 1, 0:1] for part in parts]
        centre = jnp.zeros((DIRS, 1), F32)
        for i, t in enumerate(count):
            centre = centre + d[:, first_lane + i : first_lane + i + 1] * t
        centre = centre / jnp.maximum(whole[n, KT : KT + 1, 0:1], 1.0)
        m = means(whole)
        out = [jnp.zeros((DIRS, LANES), F32) for _ in range(KT)]
        for i, t in enumerate(count):
            a = means(parts[i])
            weight = (d[:, first_lane + i : first_lane + i + 1] - centre) * t
            for k in range(KT):
                out[k] = out[k] + weight * (a[n, k : k + 1, :] - m[n, k : k + 1, :])
        return jnp.concatenate(out, axis=1)

    def between():
        each(NZ, lambda d: mz(d).wait_recv())
        chips = [sr[i] for i in range(CHIPS)]
        planes = [sz[i] for i in range(NZ)]
        every = planes[0]
        for i in range(1, NZ):
            every = every + planes[i]
        mm[chip] = means(every)
        each(CHIPS, lambda d: ma(d).start())
        lanes = lax.broadcasted_iota(I32, (DIRS, LANES), 1)
        for n in range(2):
            v = vector_of(2 * chip + n)
            out = jnp.zeros((DIRS, LANES), F32)
            for i, part in enumerate(chips + planes):
                out = jnp.where(lanes == i, dots(v, means(part), n), out)
            ds[n] = out
        over_d.start()
        over_d.wait_recv()
        both = [ds[n] + dr[n] for n in range(2)]
        inner = [scatter_of(both[n], 0, chips, sz[z], n) for n in range(2)]
        outer = [scatter_of(both[n], CHIPS, planes, every, n) for n in range(2)]
        return inner, outer

    def convert(q, i, first):
        ref = vq.at[q, i]
        scales = scales_of(vq.at[0, i])
        for n in range(2):
            j = 2 * i + n
            his, los, dots = [], [], None
            for k in range(CT):
                v = ref[CT * n + k].astype(I32)
                hi = ((v >> 8) << 8).astype(F32) * scales[n]
                lo = (v & 255).astype(F32) * scales[n]
                his.append(hi.astype(BF16))
                los.append(lo.astype(BF16))
                if not first:
                    part = (hi + lo) * mm[i, n, CT * q + k : CT * q + k + 1, :]
                    dots = part if dots is None else dots + part
            at = slice(CHUNK * q, CHUNK * (q + 1))
            vhl[j, 0:DIRS, at] = jnp.concatenate(his, axis=1)
            vhl[j, DIRS : 2 * DIRS, at] = jnp.concatenate(los, axis=1)
            if not first:
                dots = jnp.broadcast_to(jnp.sum(dots, axis=1, keepdims=True), (DIRS, LANES))
                shift[j] = dots if q == 0 else shift[j] + dots

    def receive(q, first):
        convert(q, chip, first)

        def arrived(ds):
            for d in ds:
                v_copy(q, d).wait_recv()
            for d in ds:
                convert(q, chip_from(d), first)

        grouped(arrived)

    def project(q, h, first):
        cols = slice(CHUNK * q, CHUNK * (q + 1))

        def one(t):
            at = pl.ds(pl.multiple_of(t * TILE, TILE), TILE)
            parts, shifts = [], []
            for i in range(PER):
                m = smt[h, 0, PER * t + i]
                parts.append(vhl[m, :, cols])
                if q == 1 and not first:
                    shifts.append(shift[m])
            p2 = lax.dot_general(
                jnp.concatenate(parts, axis=0), xh[h, at, cols], (((1,), (1,)), ((), ())),
                preferred_element_type=F32,
            )
            out = jnp.zeros((DIRS, TILE), F32)
            for i in range(PER):
                a = 2 * DIRS * i
                p = p2[a : a + DIRS] + p2[a + DIRS : a + 2 * DIRS]
                if q == 1 and not first:
                    p = p - jnp.concatenate([shifts[i], shifts[i]], axis=1)
                out = jnp.where(group == i, p, out)
            pc[h, :, at] = out if q == 0 else pc[h, :, at] + out

        def body(t, carry):
            one(2 * t)
            one(2 * t + 1)
            return carry

        lax.fori_loop(0, TILES // 2, body, 0)

    def p_copy(h):
        return send(pc.at[h], pr.at[h], p_s.at[h], p_r.at[h], partner)

    def expand(q, h):
        cols = slice(CHUNK * q, CHUNK * (q + 1))

        def one(t):
            at = pl.ds(pl.multiple_of(t * TILE, TILE), TILE)
            if q == 0:
                p = pc[h, :, at] + pr[h, :, at]
                hi = p.astype(BF16).astype(F32)
                lo = p - hi
                parts = []
                for i in range(PER):
                    parts.append(jnp.where(group == i, hi, 0.0).astype(BF16))
                    parts.append(jnp.where(group == i, lo, 0.0).astype(BF16))
                stack = jnp.concatenate(parts, axis=0)
                pst[h, t] = stack
            else:
                stack = pst[h, t]
            w2 = jnp.dot(stack, xh[h, at, cols], preferred_element_type=F32)
            for i in range(PER):
                a = 2 * DIRS * i
                wblk[h, PER * t + i, :, cols] = w2[a : a + DIRS] + w2[a + DIRS : a + 2 * DIRS]

        def body(t, carry):
            one(2 * t)
            one(2 * t + 1)
            return carry

        lax.fori_loop(0, TILES // 2, body, 0)

    def w_copy(n, d):
        return send(
            wq.at[n, chip_at(d)], rq.at[n, chip], rs_s.at[n, d - 1], rs_r.at[n, d - 1], plane(d)
        )

    def z_copy(step, n, d):
        ref = zq.at[step, n, z]
        return send(ref, ref, z_s.at[step, n, d - 1], z_r.at[step, n, d - 1], column(d))

    g_copy = send(gs, gr, g_s, g_r, partner)

    def total_of(j, cols):
        f0, s0 = smt[0, 1, j], smt[0, 2, j]
        f1, s1 = smt[1, 1, j], smt[1, 2, j]
        return (wblk[0, f0, :, cols] + wblk[0, s0, :, cols]) + (
            wblk[1, f1, :, cols] + wblk[1, s1, :, cols]
        )

    def node_totals(q, i, first):
        out = []
        for n in range(2):
            j = 2 * i + n
            w = total_of(j, slice(CHUNK * q, CHUNK * (q + 1)))
            if first:
                off = shift0[j] + shift1[j]
                rows = [snode[i, n, CT * q + k : CT * q + k + 1, :] for k in range(CT)]
                w = w - jnp.concatenate([off * r for r in rows], axis=1)
            out.append(w)
        return out

    def scatter_start(q, first):
        def go(ds):
            for d in ds:
                put(wq.at[q, chip_at(d)], node_totals(q, chip_at(d), first))
            for d in ds:
                w_copy(q, d).start()

        grouped(go)
        put(rq.at[q, chip], node_totals(q, chip, first))

    def term(ref):
        scales = scales_of(ref)
        return tuple(ref[k].astype(I32).astype(F32) * scales[k // CT] for k in range(2 * CT))

    def paired(acc):
        return [jnp.concatenate(acc[CT * n : CT * (n + 1)], axis=1) for n in range(2)]

    def plane_total(q):
        def body(ds, acc):
            for d in ds:
                w_copy(q, d).wait_recv()
            for d in ds:
                acc = tuple(a + b for a, b in zip(acc, term(rq.at[q, chip_from(d)])))
            return acc

        return paired(grouped(body, term(rq.at[q, chip])))

    def column_total(step, q):
        acc = term(zq.at[step, q, 0])
        for i in range(1, NZ):
            acc = tuple(a + b for a, b in zip(acc, term(zq.at[step, q, i])))
        return paired(acc)

    row_id = lax.broadcasted_iota(I32, (DIRS, 1), 0)

    def orthonormal(grams, ws):
        row = lax.broadcasted_iota(I32, (DIRS, LANES), 0)
        cols = [
            [jnp.broadcast_to(g[:, k : k + 1], (DIRS, LANES)) for k in range(DIRS)] for g in grams
        ]
        tiles = [[w[:, LANES * k : LANES * (k + 1)] for k in range(KT)] for w in ws]
        pivots = [jnp.ones((DIRS, LANES), F32) for _ in ws]
        for k in range(DIRS):
            for n in range(2):
                col = cols[n]
                pivot = col[k][k : k + 1, :]
                pivots[n] = jnp.where(row == k, pivot, pivots[n])
                f = jnp.where(row > k, col[k] * (1.0 / pivot), 0.0)
                for j in range(k + 1, DIRS):
                    col[j] = col[j] - f * col[j][k : k + 1, :]
                tiles[n] = [t - f * t[k : k + 1, :] for t in tiles[n]]
        out = []
        for n in range(2):
            scale = 1.0 / jnp.sqrt(pivots[n])
            out.append(jnp.concatenate([t * scale for t in tiles[n]], axis=1))
        return out

    def one_pass(step, first):
        for q in range(2):
            receive(q, first)
            if first and q == 1:
                offsets()
                over_h.start()
            for h in range(2):
                project(q, h, first)
                if q == 1:
                    p_copy(h).start()
            if first and q == 0:
                plane_sums()
        for h in range(2):
            p_copy(h).wait_recv()
            expand(0, h)
        if first:
            over_h.wait_recv()
        scatter_start(0, first)
        for h in range(2):
            expand(1, h)
        scatter_start(1, first)
        for q in range(2):
            each(CHIPS, lambda d: v_copy(q, d).wait_send())
        if first:
            inner, outer = between()
        for q in range(2):
            total = plane_total(q)
            if first:
                total = [total[n] + inner[n][:, CHUNK * q : CHUNK * (q + 1)] for n in range(2)]
            put(zq.at[step, q, z], total)
            each(NZ, lambda d: z_copy(step, q, d).start())
        halves = []
        for q in range(2):
            each(NZ, lambda d: z_copy(step, q, d).wait_recv())
            halves.append(column_total(step, q))
        ws = []
        for n in range(2):
            w = jnp.concatenate([halves[0][n], halves[1][n]], axis=1)
            if first:
                w = w + outer[n]
            w = w / jnp.concatenate([mm[chip, n, KT : KT + 1, :]] * KT, axis=1)
            ws.append(w)
            gs[n, :, 0:DIRS] = lax.dot_general(
                w, w, (((1,), (1,)), ((), ())), precision=lax.Precision.HIGHEST,
                preferred_element_type=F32,
            )
        g_copy.start()
        g_copy.wait_recv()
        vectors = orthonormal([gs[n, :, 0:DIRS] + gr[n, :, 0:DIRS] for n in range(2)], ws)
        put_whole(vq, chip, vectors)
        for q in range(2):
            gather_start(q)
        for n in range(2):
            vout[n] = vectors[n]
        if first:
            each(CHIPS, lambda d: ma(d).wait_recv())
        g_copy.wait_send()
        for n in range(2):
            p_copy(n).wait_send()
            each(CHIPS, lambda d: w_copy(n, d).wait_send())
            each(NZ, lambda d: z_copy(step, n, d).wait_send())

    one_pass(0, True)

    def later(step, carry):
        one_pass(step, False)
        return carry

    lax.fori_loop(1, PASSES, later, 0)

    over_o = send(vout.at[other], vin, o_s, o_r, partner)
    over_o.start()
    dirs[:, mine] = vout[c]
    for q in range(2):
        receive(q, False)
        project(q, other, False)
        if q == 1:
            p_copy(other).start()
        project(q, c, False)
    over_o.wait_recv()
    dirs[:, theirs] = vin[...]
    back = send(pc.at[other], pr.at[c], p_s.at[other], p_r.at[c], partner)
    back.wait_recv()
    coords[...] = (pc[c] + pr[c]).astype(BF16)
    back.wait_send()
    for cp in (over_o, over_v, over_m, over_x, over_h, over_d):
        cp.wait_send()
    for n in range(2):
        each(CHIPS, lambda d: v_copy(n, d).wait_send())
    each(CHIPS, lambda d: ms(d).wait_send())
    each(CHIPS, lambda d: ma(d).wait_send())
    each(NZ, lambda d: mz(d).wait_send())


def on_device(embeddings, membership, start):
    member = membership.reshape(1, BLOCKS)
    vmem = pl.BlockSpec(memory_space=pltpu.VMEM)
    hbm = pl.BlockSpec(memory_space=pltpu.HBM)
    dma = pltpu.SemaphoreType.DMA
    dirs, coords = pl.pallas_call(
        kernel,
        out_shape=(
            jax.ShapeDtypeStruct((DIRS, D), F32),
            jax.ShapeDtypeStruct((DIRS, ROWS), BF16),
        ),
        in_specs=[hbm, hbm, hbm],
        out_specs=(vmem, vmem),
        scratch_shapes=[
            pltpu.VMEM((2, ROWS, HALF), BF16),
            pltpu.SMEM((2, 8, LANES), I32),
            pltpu.SMEM((2, 1, BLOCKS), I32),
            pltpu.VMEM((2, 1, BLOCKS), I32),
            pltpu.VMEM((2, 8, LANES), I32),
            pltpu.VMEM((DIRS, D), F32),
            pltpu.VMEM((DIRS, HALF), F32),
            pltpu.VMEM((2, CHIPS, KT + 1, DIRS, LANES), I16),
            pltpu.VMEM((32, 2 * DIRS, HALF), BF16),
            pltpu.VMEM((32, DIRS, LANES), F32),
            pltpu.VMEM((32, DIRS, LANES), F32),
            pltpu.VMEM((32, DIRS, LANES), F32),
            pltpu.VMEM((2, DIRS, ROWS), F32),
            pltpu.VMEM((2, DIRS, ROWS), F32),
            pltpu.VMEM((2, TILES, 2 * DIRS * PER, TILE), BF16),
            pltpu.VMEM((2, BLOCKS + 1, DIRS, HALF), F32),
            pltpu.VMEM((2, CHIPS, KT + 1, DIRS, LANES), I16),
            pltpu.VMEM((2, CHIPS, KT + 1, DIRS, LANES), I16),
            pltpu.VMEM((PASSES, 2, NZ, KT + 1, DIRS, LANES), I16),
            pltpu.VMEM((2, DIRS, LANES), F32),
            pltpu.VMEM((2, DIRS, LANES), F32),
            pltpu.VMEM((2, DIRS, HALF), F32),
            pltpu.VMEM((DIRS, HALF), F32),
            pltpu.VMEM((2, BLOCKS + 1, 8, LANES), F32),
            pltpu.VMEM((CHIPS, 2, 8, LANES), F32),
            pltpu.VMEM((CHIPS, 2, 8, LANES), F32),
            pltpu.VMEM((NZ, 2, 8, LANES), F32),
            pltpu.VMEM((CHIPS, 2, 8, LANES), F32),
            pltpu.VMEM((2, DIRS, LANES), F32),
            pltpu.VMEM((2, DIRS, LANES), F32),
            dma, dma, dma, dma, dma, dma, dma, dma, dma, dma, dma, dma, dma,
            dma((2, 15)), dma((2, 15)),
            dma((2,)), dma((2,)),
            dma((2, 15)), dma((2, 15)),
            dma((PASSES, 2, 7)), dma((PASSES, 2, 7)),
            dma, dma,
            dma((15,)), dma((15,)), dma((7,)), dma((7,)), dma((15,)), dma((15,)),
            dma, dma, dma, dma,
        ],
        compiler_params=pltpu.CompilerParams(
            collective_id=0, has_side_effects=True, vmem_limit_bytes=52 * 1024 * 1024
        ),
    )(member, embeddings, start)
    return (dirs[None], coords)


def solution(mesh):
    return jax.shard_map(
        on_device,
        mesh=mesh,
        in_specs=(P(("node", "rows"), None), P(("node", "rows"), None), P("node", None, None)),
        out_specs=(P("node", None, None), P(None, ("node", "rows"))),
        check_vma=False,
    )
```

```python
import jax
import jax.numpy as jnp
from jax import lax
from jax.experimental import pallas as pl
from jax.experimental.pallas import tpu as pltpu
from jax.sharding import PartitionSpec as P

PASSES = 3
MESH = pl.DeviceIdType.MESH
F32 = jnp.float32
BF16 = jnp.bfloat16
I16 = jnp.int16
I32 = jnp.int32

DIRS = 16
D = 1024
HALF = 512
LANES = 128
KT = HALF // LANES
CHUNK = 256
CT = CHUNK // LANES
ROWS = 2048
BLOCK = 64
BLOCKS = 32
TILE = 256
PER = TILE // BLOCK
TILES = ROWS // TILE
CHIPS = 16
NZ = 8
FAR_FIRST = (10, 6, 9, 11, 14, 5, 7, 13, 15, 2, 8, 1, 3, 4, 12)


def lane_half():
    return lax.broadcasted_iota(I32, (DIRS, LANES), 1) < LANES // 2


def put(ref, pair):
    exponents = []
    for n, w in enumerate(pair):
        tiles = [w[:, LANES * k : LANES * (k + 1)] for k in range(CT)]
        top = jnp.maximum(jnp.abs(tiles[0]), jnp.abs(tiles[1]))
        top = jnp.maximum(jnp.max(top, axis=1, keepdims=True), 1e-30)
        e = jnp.floor(jnp.log2(top))
        scale = jnp.exp2(14.0 - e)
        for k in range(CT):
            q = jnp.clip(jnp.round(tiles[k] * scale), -32767.0, 32767.0)
            ref[CT * n + k] = q.astype(I32).astype(I16)
        exponents.append(jnp.broadcast_to(e.astype(I32), (DIRS, LANES)))
    ref[2 * CT] = jnp.where(lane_half(), exponents[0], exponents[1]).astype(I16)


def put_whole(ref, chip, pair):
    exponents = []
    for n, w in enumerate(pair):
        tiles = [w[:, LANES * k : LANES * (k + 1)] for k in range(KT)]
        top = jnp.maximum(
            jnp.maximum(jnp.abs(tiles[0]), jnp.abs(tiles[1])),
            jnp.maximum(jnp.abs(tiles[2]), jnp.abs(tiles[3])),
        )
        top = jnp.maximum(jnp.max(top, axis=1, keepdims=True), 1e-30)
        e = jnp.floor(jnp.log2(top))
        scale = jnp.exp2(14.0 - e)
        for k in range(KT):
            q = jnp.clip(jnp.round(tiles[k] * scale), -32767.0, 32767.0)
            ref[k // CT, chip, CT * n + k % CT] = q.astype(I32).astype(I16)
        exponents.append(jnp.broadcast_to(e.astype(I32), (DIRS, LANES)))
    ref[0, chip, 2 * CT] = jnp.where(lane_half(), exponents[0], exponents[1]).astype(I16)


def scales_of(ref):
    s = jnp.exp2(ref[2 * CT].astype(I32).astype(F32) - 14.0)
    return [jnp.broadcast_to(s[:, LANES // 2 * n : LANES // 2 * n + 1], (DIRS, LANES)) for n in range(2)]


def kernel(
    member, x_hbm, start, dirs, coords,
    xh, smt, smm, mv, tab, vs, vr, vq, vhl, shift, shift0, shift1, pc, pr, pst, wblk, wq, rq, zq, gs, gr, vout, vin,
    sblk, snode, sr, sz, mm, ds, dr,
    xsem, xs, xr, msem, mss, msr, nsem, tsem, vsem, vss, vsr, h_s, h_r, ag_s, ag_r, p_s, p_r, rs_s, rs_r, z_s, z_r, g_s, g_r,
    ms_s, ms_r, mz_s, mz_r, ma_s, ma_r, d_s, d_r, o_s, o_r,
):
    me = lax.axis_index("node")
    z = lax.axis_index("rows")
    x, y, c = me >> 3, (me >> 1) & 3, me & 1
    chip = me >> 1
    other = 1 - c

    def chip_at(d):
        return (((x + (d >> 2)) & 3) << 2) + ((y + d) & 3)

    def chip_from(d):
        return (((x + 4 - (d >> 2)) & 3) << 2) + ((y + 4 - (d & 3)) & 3)

    def plane(d):
        return (chip_at(d) * 2 + c, z)

    def column(d):
        return (me, (z + d) & (NZ - 1))

    partner = (chip * 2 + other, z)

    def send(src, dst, ssem, rsem, to):
        return pltpu.make_async_remote_copy(
            src_ref=src, dst_ref=dst, send_sem=ssem, recv_sem=rsem, device_id=to, device_id_type=MESH
        )

    def each(n, what):
        if n == NZ:
            for d in (4, 3, 5, 2, 6, 1, 7):
                what(d)
        else:
            grouped(lambda ds: [what(d) for d in ds])

    def grouped(what, carry=0, order=FAR_FIRST):
        for g in range(0, CHIPS - 1, 5):
            ds = order[g : g + 5]
            if isinstance(carry, int):
                what(ds)
            else:
                carry = what(ds, carry)
        return carry

    mine = pl.ds(pl.multiple_of(c * HALF, HALF), HALF)
    theirs = pl.ds(pl.multiple_of(other * HALF, HALF), HALF)
    barrier = pltpu.get_barrier_semaphore()

    def greet_plane(d):
        pl.semaphore_signal(barrier, inc=1, device_id=plane(d), device_id_type=MESH)

    def greet_column(d):
        pl.semaphore_signal(barrier, inc=1, device_id=column(d), device_id_type=MESH)

    each(NZ, greet_column)
    each(CHIPS, greet_plane)
    pl.semaphore_signal(barrier, inc=1, device_id=partner, device_id_type=MESH)

    load = pltpu.make_async_copy(x_hbm.at[:, mine], xh.at[c], xsem)
    load.start()
    load_m = pltpu.make_async_copy(member, mv.at[c], msem)
    load_m.start()
    load_v = pltpu.make_async_copy(start.at[0], vs, vsem)
    load_v.start()


    group = lax.broadcasted_iota(I32, (DIRS, TILE), 1) >> 6
    ones_rows = (lax.broadcasted_iota(I32, (DIRS, TILE), 0) == group).astype(F32).astype(BF16)

    def sum_tiles(h):
        def body(t, carry):
            tile = xh[h, pl.ds(pl.multiple_of(t * TILE, TILE), TILE), :]
            s = jnp.dot(ones_rows, tile, preferred_element_type=F32)
            for i in range(PER):
                rows = [s[i : i + 1, LANES * k : LANES * (k + 1)] for k in range(KT)]
                rows.append(jnp.full((1, LANES), float(BLOCK), F32))
                rows.append(jnp.zeros((3, LANES), F32))
                sblk[h, PER * t + i] = jnp.concatenate(rows, axis=0)
            return carry

        lax.fori_loop(0, TILES, body, 0)

    wblk[0, BLOCKS] = jnp.zeros((DIRS, HALF), F32)
    wblk[1, BLOCKS] = jnp.zeros((DIRS, HALF), F32)
    sblk[0, BLOCKS] = jnp.zeros((8, LANES), F32)
    sblk[1, BLOCKS] = jnp.zeros((8, LANES), F32)
    load_v.wait()
    load_m.wait()

    pl.semaphore_wait(barrier, 1 + (CHIPS - 1) + (NZ - 1))

    over_v = send(vs.at[:, theirs], vr, vss, vsr, partner)
    over_v.start()
    over_m = send(mv.at[c], mv.at[c], mss, msr, partner)
    over_m.start()
    over_x = send(x_hbm.at[:, theirs], xh.at[c], xs, xr, partner)
    over_x.start()

    def v_copy(n, d):
        ref = vq.at[n, chip] if n == 0 else vq.at[n, chip, pl.ds(0, 2 * CT)]
        return send(ref, ref, ag_s.at[n, d - 1], ag_r.at[n, d - 1], plane(d))

    def gather_start(n):
        each(CHIPS, lambda d: v_copy(n, d).start())

    over_v.wait_recv()
    own, pair = vs[:, mine], vr[...]
    put_whole(vq, chip, [jnp.where(c == 0, own, pair), jnp.where(c == 0, pair, own)])
    for q in range(2):
        gather_start(q)

    load.wait()
    sum_tiles(c)
    over_m.wait_recv()
    names = pltpu.make_async_copy(mv, smm, nsem)
    names.start()
    names.wait()
    lane = lax.broadcasted_iota(I32, (1, LANES), 1)
    for h in range(2):
        low = jnp.full((1, LANES), BLOCKS, I32)
        high = low
        hits = jnp.zeros((1, LANES), I32)
        for b in range(BLOCKS):
            hit = lane == smm[h, 0, b]
            low = jnp.where(hit & (hits == 0), b, low)
            high = jnp.where(hit & (hits > 0), b, high)
            hits = jnp.where(hit, hits + 1, hits)
        row = jnp.concatenate([mv[h], jnp.zeros((1, LANES - BLOCKS), I32)], axis=1)
        tab[h] = jnp.concatenate([row, low, high, jnp.zeros((5, LANES), I32)], axis=0)
    move = pltpu.make_async_copy(tab, smt, tsem)
    move.start()
    over_x.wait_recv()
    sum_tiles(other)
    move.wait()

    def total(ref, j):
        f0, s0 = smt[0, 1, j], smt[0, 2, j]
        f1, s1 = smt[1, 1, j], smt[1, 2, j]
        return (ref[0, f0] + ref[0, s0]) + (ref[1, f1] + ref[1, s1])

    def node_sums(i, carry):
        for n in range(2):
            snode[i, n] = total(sblk, 2 * i + n)
        return carry

    lax.fori_loop(0, CHIPS, node_sums, 0)
    sr[chip] = snode[chip]

    def ms(d):
        return send(snode.at[chip_at(d)], sr.at[chip], ms_s.at[d - 1], ms_r.at[d - 1], plane(d))

    def mz(d):
        return send(sz.at[z], sz.at[z], mz_s.at[d - 1], mz_r.at[d - 1], column(d))

    def ma(d):
        return send(mm.at[chip], mm.at[chip], ma_s.at[d - 1], ma_r.at[d - 1], plane(d))

    each(CHIPS, lambda d: ms(d).start())

    tile_row = lax.broadcasted_iota(I32, (2, 8, LANES), 1)

    def means(a):
        return jnp.where(tile_row < KT, a / jnp.maximum(a[:, KT : KT + 1, :], 1.0), a)

    def plane_sums():
        each(CHIPS, lambda d: ms(d).wait_recv())
        acc = sr[0]
        for i in range(1, CHIPS):
            acc = acc + sr[i]
        sz[z] = acc
        each(NZ, lambda d: mz(d).start())

    def dots(v, a, n):
        out = None
        for k in range(KT):
            part = v[:, LANES * k : LANES * (k + 1)] * a[n, k : k + 1, :]
            out = part if out is None else out + part
        return jnp.sum(out, axis=1, keepdims=True)

    def vector_of(j):
        return vhl[j, 0:DIRS, :].astype(F32) + vhl[j, DIRS : 2 * DIRS, :].astype(F32)

    def offsets():
        def body(g, carry):
            for i in (4 * g, 4 * g + 1, 4 * g + 2, 4 * g + 3):
                a = means(snode[i])
                for n in range(2):
                    shift0[2 * i + n] = jnp.broadcast_to(dots(vector_of(2 * i + n), a, n), (DIRS, LANES))
            return carry

        lax.fori_loop(0, CHIPS // 4, body, 0)

    over_h = send(shift0, shift1, h_s, h_r, partner)
    over_d = send(ds, dr, d_s, d_r, partner)

    def scatter_of(d, first_lane, parts, whole, n):
        count = [part[n, KT : KT + 1, 0:1] for part in parts]
        centre = jnp.zeros((DIRS, 1), F32)
        for i, t in enumerate(count):
            centre = centre + d[:, first_lane + i : first_lane + i + 1] * t
        centre = centre / jnp.maximum(whole[n, KT : KT + 1, 0:1], 1.0)
        m = means(whole)
        out = [jnp.zeros((DIRS, LANES), F32) for _ in range(KT)]
        for i, t in enumerate(count):
            a = means(parts[i])
            weight = (d[:, first_lane + i : first_lane + i + 1] - centre) * t
            for k in range(KT):
                out[k] = out[k] + weight * (a[n, k : k + 1, :] - m[n, k : k + 1, :])
        return jnp.concatenate(out, axis=1)

    def between():
        each(NZ, lambda d: mz(d).wait_recv())
        chips = [sr[i] for i in range(CHIPS)]
        planes = [sz[i] for i in range(NZ)]
        every = planes[0]
        for i in range(1, NZ):
            every = every + planes[i]
        mm[chip] = means(every)
        each(CHIPS, lambda d: ma(d).start())
        lanes = lax.broadcasted_iota(I32, (DIRS, LANES), 1)
        for n in range(2):
            v = vector_of(2 * chip + n)
            out = jnp.zeros((DIRS, LANES), F32)
            for i, part in enumerate(chips + planes):
                out = jnp.where(lanes == i, dots(v, means(part), n), out)
            ds[n] = out
        over_d.start()
        over_d.wait_recv()
        both = [ds[n] + dr[n] for n in range(2)]
        inner = [scatter_of(both[n], 0, chips, sz[z], n) for n in range(2)]
        outer = [scatter_of(both[n], CHIPS, planes, every, n) for n in range(2)]
        return inner, outer

    def convert(q, i, first):
        ref = vq.at[q, i]
        scales = scales_of(vq.at[0, i])
        for n in range(2):
            j = 2 * i + n
            his, los, dots = [], [], None
            for k in range(CT):
                v = ref[CT * n + k].astype(I32)
                hi = ((v >> 8) << 8).astype(F32) * scales[n]
                lo = (v & 255).astype(F32) * scales[n]
                his.append(hi.astype(BF16))
                los.append(lo.astype(BF16))
                if not first:
                    part = (hi + lo) * mm[i, n, CT * q + k : CT * q + k + 1, :]
                    dots = part if dots is None else dots + part
            at = slice(CHUNK * q, CHUNK * (q + 1))
            vhl[j, 0:DIRS, at] = jnp.concatenate(his, axis=1)
            vhl[j, DIRS : 2 * DIRS, at] = jnp.concatenate(los, axis=1)
            if not first:
                dots = jnp.broadcast_to(jnp.sum(dots, axis=1, keepdims=True), (DIRS, LANES))
                shift[j] = dots if q == 0 else shift[j] + dots

    def receive(q, first):
        convert(q, chip, first)

        def arrived(ds):
            for d in ds:
                v_copy(q, d).wait_recv()
            for d in ds:
                convert(q, chip_from(d), first)

        grouped(arrived, order=FAR_FIRST[::-1])

    def project(q, h, first):
        cols = slice(CHUNK * q, CHUNK * (q + 1))

        def one(t):
            at = pl.ds(t * TILE, TILE)
            parts, shifts = [], []
            for i in range(PER):
                m = smt[h, 0, PER * t + i]
                parts.append(vhl[m, :, cols])
                if q == 1 and not first:
                    shifts.append(shift[m])
            p2 = lax.dot_general(
                jnp.concatenate(parts, axis=0), xh[h, at, cols], (((1,), (1,)), ((), ())),
                preferred_element_type=F32,
            )
            out = jnp.zeros((DIRS, TILE), F32)
            for i in range(PER):
                a = 2 * DIRS * i
                p = p2[a : a + DIRS] + p2[a + DIRS : a + 2 * DIRS]
                if q == 1 and not first:
                    p = p - jnp.concatenate([shifts[i], shifts[i]], axis=1)
                out = jnp.where(group == i, p, out)
            pc[h, :, at] = out if q == 0 else pc[h, :, at] + out

        for t in range(TILES):
            one(t)

    def p_copy(h):
        return send(pc.at[h], pr.at[h], p_s.at[h], p_r.at[h], partner)

    def expand(q, h):
        cols = slice(CHUNK * q, CHUNK * (q + 1))

        def one(t):
            at = pl.ds(pl.multiple_of(t * TILE, TILE), TILE)
            if q == 0:
                p = pc[h, :, at] + pr[h, :, at]
                hi = p.astype(BF16).astype(F32)
                lo = p - hi
                parts = []
                for i in range(PER):
                    parts.append(jnp.where(group == i, hi, 0.0).astype(BF16))
                    parts.append(jnp.where(group == i, lo, 0.0).astype(BF16))
                stack = jnp.concatenate(parts, axis=0)
                pst[h, t] = stack
            else:
                stack = pst[h, t]
            w2 = jnp.dot(stack, xh[h, at, cols], preferred_element_type=F32)
            for i in range(PER):
                a = 2 * DIRS * i
                wblk[h, PER * t + i, :, cols] = w2[a : a + DIRS] + w2[a + DIRS : a + 2 * DIRS]

        for t in range(TILES):
            one(t)

    def w_copy(n, d):
        return send(
            wq.at[n, chip_at(d)], rq.at[n, chip], rs_s.at[n, d - 1], rs_r.at[n, d - 1], plane(d)
        )

    def z_copy(step, n, d):
        ref = zq.at[step, n, z]
        return send(ref, ref, z_s.at[step, n, d - 1], z_r.at[step, n, d - 1], column(d))

    g_copy = send(gs, gr, g_s, g_r, partner)

    def total_of(j, cols):
        f0, s0 = smt[0, 1, j], smt[0, 2, j]
        f1, s1 = smt[1, 1, j], smt[1, 2, j]
        return (wblk[0, f0, :, cols] + wblk[0, s0, :, cols]) + (
            wblk[1, f1, :, cols] + wblk[1, s1, :, cols]
        )

    def node_totals(q, i, first):
        out = []
        for n in range(2):
            j = 2 * i + n
            w = total_of(j, slice(CHUNK * q, CHUNK * (q + 1)))
            if first:
                off = shift0[j] + shift1[j]
                rows = [snode[i, n, CT * q + k : CT * q + k + 1, :] for k in range(CT)]
                w = w - jnp.concatenate([off * r for r in rows], axis=1)
            out.append(w)
        return out

    def scatter_start(q, first):
        def go(ds):
            for d in ds:
                put(wq.at[q, chip_at(d)], node_totals(q, chip_at(d), first))
            for d in ds:
                w_copy(q, d).start()

        grouped(go)
        put(rq.at[q, chip], node_totals(q, chip, first))

    def term(ref):
        scales = scales_of(ref)
        return tuple(ref[k].astype(I32).astype(F32) * scales[k // CT] for k in range(2 * CT))

    def paired(acc):
        return [jnp.concatenate(acc[CT * n : CT * (n + 1)], axis=1) for n in range(2)]

    def plane_total(q):
        def body(ds, acc):
            for d in ds:
                w_copy(q, d).wait_recv()
            for d in ds:
                acc = tuple(a + b for a, b in zip(acc, term(rq.at[q, chip_from(d)])))
            return acc

        return paired(grouped(body, term(rq.at[q, chip]), FAR_FIRST[::-1]))

    def column_total(step, q):
        acc = term(zq.at[step, q, 0])
        for i in range(1, NZ):
            acc = tuple(a + b for a, b in zip(acc, term(zq.at[step, q, i])))
        return paired(acc)

    row_id = lax.broadcasted_iota(I32, (DIRS, 1), 0)

    def orthonormal(grams, ws):
        row = lax.broadcasted_iota(I32, (DIRS, LANES), 0)
        cols = [
            [jnp.broadcast_to(g[:, k : k + 1], (DIRS, LANES)) for k in range(DIRS)] for g in grams
        ]
        tiles = [[w[:, LANES * k : LANES * (k + 1)] for k in range(KT)] for w in ws]
        pivots = [jnp.ones((DIRS, LANES), F32) for _ in ws]
        for k in range(DIRS):
            for n in range(2):
                col = cols[n]
                pivot = col[k][k : k + 1, :]
                pivots[n] = jnp.where(row == k, pivot, pivots[n])
                f = jnp.where(row > k, col[k] * (1.0 / pivot), 0.0)
                for j in range(k + 1, DIRS):
                    col[j] = col[j] - f * col[j][k : k + 1, :]
                tiles[n] = [t - f * t[k : k + 1, :] for t in tiles[n]]
        out = []
        for n in range(2):
            scale = 1.0 / jnp.sqrt(pivots[n])
            out.append(jnp.concatenate([t * scale for t in tiles[n]], axis=1))
        return out

    def one_pass(step, first):
        for q in range(2):
            receive(q, first)
            if first and q == 1:
                offsets()
                over_h.start()
            for h in range(2):
                project(q, h, first)
                if q == 1:
                    p_copy(h).start()
            if first and q == 0:
                plane_sums()
        for h in range(2):
            p_copy(h).wait_recv()
            expand(0, h)
        if first:
            over_h.wait_recv()
        scatter_start(0, first)
        for h in range(2):
            expand(1, h)
        scatter_start(1, first)
        for q in range(2):
            each(CHIPS, lambda d: v_copy(q, d).wait_send())
        if first:
            inner, outer = between()
        for q in range(2):
            total = plane_total(q)
            if first:
                total = [total[n] + inner[n][:, CHUNK * q : CHUNK * (q + 1)] for n in range(2)]
            put(zq.at[step, q, z], total)
            each(NZ, lambda d: z_copy(step, q, d).start())
        halves = []
        for q in range(2):
            each(NZ, lambda d: z_copy(step, q, d).wait_recv())
            halves.append(column_total(step, q))
        ws = []
        for n in range(2):
            w = jnp.concatenate([halves[0][n], halves[1][n]], axis=1)
            if first:
                w = w + outer[n]
            w = w / jnp.concatenate([mm[chip, n, KT : KT + 1, :]] * KT, axis=1)
            ws.append(w)
            gs[n, :, 0:DIRS] = lax.dot_general(
                w, w, (((1,), (1,)), ((), ())), precision=lax.Precision.HIGHEST,
                preferred_element_type=F32,
            )
        g_copy.start()
        g_copy.wait_recv()
        vectors = orthonormal([gs[n, :, 0:DIRS] + gr[n, :, 0:DIRS] for n in range(2)], ws)
        put_whole(vq, chip, vectors)
        for q in range(2):
            gather_start(q)
        for n in range(2):
            vout[n] = vectors[n]
        if first:
            each(CHIPS, lambda d: ma(d).wait_recv())
        g_copy.wait_send()
        for n in range(2):
            p_copy(n).wait_send()
            each(CHIPS, lambda d: w_copy(n, d).wait_send())
            each(NZ, lambda d: z_copy(step, n, d).wait_send())

    one_pass(0, True)

    def later(step, carry):
        one_pass(step, False)
        return carry

    lax.fori_loop(1, PASSES, later, 0)

    over_o = send(vout.at[other], vin, o_s, o_r, partner)
    over_o.start()
    dirs[:, mine] = vout[c]
    for cp in (over_v, over_m, over_x, over_h, over_d):
        cp.wait_send()
    each(CHIPS, lambda d: ms(d).wait_send())
    each(CHIPS, lambda d: ma(d).wait_send())
    each(NZ, lambda d: mz(d).wait_send())
    for q in range(2):
        receive(q, False)
        project(q, other, False)
        if q == 1:
            p_copy(other).start()
        project(q, c, False)
    over_o.wait_recv()
    dirs[:, theirs] = vin[...]
    back = send(pc.at[other], pr.at[c], p_s.at[other], p_r.at[c], partner)
    for q in range(2):
        each(CHIPS, lambda d: v_copy(q, d).wait_send())
    back.wait_recv()
    coords[...] = (pc[c] + pr[c]).astype(BF16)
    back.wait_send()
    over_o.wait_send()


def on_device(embeddings, membership, start):
    member = membership.reshape(1, BLOCKS)
    vmem = pl.BlockSpec(memory_space=pltpu.VMEM)
    hbm = pl.BlockSpec(memory_space=pltpu.HBM)
    dma = pltpu.SemaphoreType.DMA
    dirs, coords = pl.pallas_call(
        kernel,
        out_shape=(
            jax.ShapeDtypeStruct((DIRS, D), F32),
            jax.ShapeDtypeStruct((DIRS, ROWS), BF16),
        ),
        in_specs=[hbm, hbm, hbm],
        out_specs=(vmem, vmem),
        scratch_shapes=[
            pltpu.VMEM((2, ROWS, HALF), BF16),
            pltpu.SMEM((2, 8, LANES), I32),
            pltpu.SMEM((2, 1, BLOCKS), I32),
            pltpu.VMEM((2, 1, BLOCKS), I32),
            pltpu.VMEM((2, 8, LANES), I32),
            pltpu.VMEM((DIRS, D), F32),
            pltpu.VMEM((DIRS, HALF), F32),
            pltpu.VMEM((2, CHIPS, KT + 1, DIRS, LANES), I16),
            pltpu.VMEM((32, 2 * DIRS, HALF), BF16),
            pltpu.VMEM((32, DIRS, LANES), F32),
            pltpu.VMEM((32, DIRS, LANES), F32),
            pltpu.VMEM((32, DIRS, LANES), F32),
            pltpu.VMEM((2, DIRS, ROWS), F32),
            pltpu.VMEM((2, DIRS, ROWS), F32),
            pltpu.VMEM((2, TILES, 2 * DIRS * PER, TILE), BF16),
            pltpu.VMEM((2, BLOCKS + 1, DIRS, HALF), F32),
            pltpu.VMEM((2, CHIPS, KT + 1, DIRS, LANES), I16),
            pltpu.VMEM((2, CHIPS, KT + 1, DIRS, LANES), I16),
            pltpu.VMEM((PASSES, 2, NZ, KT + 1, DIRS, LANES), I16),
            pltpu.VMEM((2, DIRS, LANES), F32),
            pltpu.VMEM((2, DIRS, LANES), F32),
            pltpu.VMEM((2, DIRS, HALF), F32),
            pltpu.VMEM((DIRS, HALF), F32),
            pltpu.VMEM((2, BLOCKS + 1, 8, LANES), F32),
            pltpu.VMEM((CHIPS, 2, 8, LANES), F32),
            pltpu.VMEM((CHIPS, 2, 8, LANES), F32),
            pltpu.VMEM((NZ, 2, 8, LANES), F32),
            pltpu.VMEM((CHIPS, 2, 8, LANES), F32),
            pltpu.VMEM((2, DIRS, LANES), F32),
            pltpu.VMEM((2, DIRS, LANES), F32),
            dma, dma, dma, dma, dma, dma, dma, dma, dma, dma, dma, dma, dma,
            dma((2, 15)), dma((2, 15)),
            dma((2,)), dma((2,)),
            dma((2, 15)), dma((2, 15)),
            dma((PASSES, 2, 7)), dma((PASSES, 2, 7)),
            dma, dma,
            dma((15,)), dma((15,)), dma((7,)), dma((7,)), dma((15,)), dma((15,)),
            dma, dma, dma, dma,
        ],
        compiler_params=pltpu.CompilerParams(
            collective_id=0, has_side_effects=True, vmem_limit_bytes=52 * 1024 * 1024
        ),
    )(member, embeddings, start)
    return (dirs[None], coords)


def solution(mesh):
    return jax.shard_map(
        on_device,
        mesh=mesh,
        in_specs=(P(("node", "rows"), None), P(("node", "rows"), None), P("node", None, None)),
        out_specs=(P("node", None, None), P(None, ("node", "rows"))),
        check_vma=False,
    )
```
